128 devices in a mesh: row: 4 (over x), col: 32 (over z, y, core).
Axes of the slice: x: 4, y: 4, z: 4, core: 2. Of those that a mesh axis runs over, the one named last changes fastest.
Arguments:
- stiffness: bfloat16 [160, 1024, 1024], P('col', 'row'), may hold values from -0.1875 to 0.1875
- coupling: bfloat16 [160, 1024, 2, 768], P('col', 'row'), may hold values from -1.0546875 to 1.0546875
- slave_diag: float32 [160, 1024], P('col', 'row'), may hold values from 0.5 to 2
- slave_masters: int32 [160, 2], P('col'), may hold values from 0 to 31, all different within a row; in each aligned block of 5 rows (0 to 4, 5 to 9, ...) at most 2 rows name the same one
Outputs:
- cross_fill: bfloat16 [160, 768, 768], P('col', 'row')
- diag_fill: bfloat16 [32, 768, 768], P('col', 'row')
The draws below stay inside these ranges and needn't reach their ends.
Inputs may be any that keep to these rules, and one draw needn't show every extreme that they name: `slave_masters`: each slave block names two different master blocks; among the slave blocks of one index of col no master block is named more than 2 times, and some master block is named exactly 2 times; every master block is named somewhere.
All inputs are finite; a program needn't handle non-finite values.
Results may differ from the reference program's by a relative error of at most 0.0071.
Values may be sent and summed in bfloat16 or wider, within the bound.
A program may use at most 192 MiB of HBM per device.

```python
import math
import jax
import jax.numpy as jnp
import numpy as np
from jax import lax

FW = 768
NS = 1024
SB_DEV = 5
MOST = 2
SLAVES = 160
MASTERS = 32
N_COL = 32


def shard_levels(own_key, dims, split, low, top_value):
    level = 1.0
    for axis_at, parts in split:
        draws = jax.random.uniform(jax.random.fold_in(jax.random.fold_in(own_key, 6), axis_at), (parts,), jnp.float32, low / len(split), top_value / len(split))
        level = level * jnp.repeat(jnp.exp(draws), dims[axis_at] // parts).reshape((-1,) + (1,) * (len(dims) - 1 - axis_at))
    return level


def routed_block(rng, own, number, rows, amount, top, reach, slope):
    order = jax.random.permutation(rng, amount)
    crowded, common = load_shares(amount, rows * top, reach, slope, True), load_shares(amount, rows * top, reach, slope, False)
    places = jnp.arange(amount)

    def named(lengths, turn):
        used = int((lengths > 0).sum())
        fixed = max(1, used // 4)
        shifted = fixed + (places - fixed + turn * (used - fixed)) % max(1, amount - fixed)
        return jnp.zeros((amount,), jnp.int32).at[order[jnp.where(places < fixed, places, shifted)]].set(jnp.asarray(lengths, jnp.int32))

    lengths = jnp.where(number % 4 == 0, named(crowded, number // 4), named(common, number - number // 4 - 1))
    mixed = jax.random.permutation(jax.random.fold_in(own, 3), amount)
    source_of, taker = mixed[0:amount // 2 * 2:2], mixed[1:amount // 2 * 2:2]
    slack = jnp.minimum(lengths[source_of] - 1, reach - lengths[taker]) // 2
    slack = jnp.where((source_of == order[0]) | (taker == order[0]) | (lengths[taker] == 0), 0, jnp.maximum(slack, 0))
    shifted = jax.random.randint(jax.random.fold_in(own, 4), (amount // 2,), 0, 1 << 20) % (slack + 1)
    lengths = lengths.at[source_of].add(-shifted).at[taker].add(shifted)
    items = jnp.searchsorted(jnp.cumsum(lengths), jnp.arange(rows * top), side="right").astype(jnp.int32)
    listing = items.reshape(top, rows).T
    listing = listing[jax.random.permutation(jax.random.fold_in(own, 1), rows)]
    turn = jax.random.randint(jax.random.fold_in(own, 2), (rows, 1), 0, top)
    return jnp.take_along_axis(listing, (jnp.arange(top)[None, :] + turn) % top, axis=1)


def load_shares(amount, total, reach, slope, full):
    portions = [(1 << 20) // math.isqrt(rank ** slope) + 1 for rank in range(1, amount + 1)]
    largest = reach if full else min(reach, max(-(-total // amount), total * portions[0] // sum(portions)))
    least = 1 if total - largest >= amount - 1 else 0
    given, spare = [largest] + [least] * (amount - 1), total - largest - least * (amount - 1)
    while spare > 0:
        candidates = [i for i in range(1, amount) if given[i] < largest] or [i for i in range(1, amount) if given[i] < reach]
        pool, remaining = sum([portions[i] for i in candidates]), spare
        for i in candidates:
            extra = min(reach - given[i], max(1, remaining * portions[i] // pool), spare)
            given[i] = given[i] + extra
            spare = spare - extra
    return np.array(given)


def bell_draw(key, extent, deviation, limit, shards=(), kind=jnp.bfloat16):
    values = jax.random.normal(key, extent, jnp.float32) * deviation
    if len(shards) > 0:
        values = shard_levels(key, extent, shards, -0.22, 0.18) * values
    return jnp.clip(values, min=-limit, max=limit).astype(kind)


def setup_inputs(seed: int = 0) -> dict:
    seeds = jax.random.split(jax.random.key(seed), 5)
    stiffness = bell_draw(seeds[0], (SLAVES, NS, NS), NS ** -0.5, 0.1875, ((0, 32), (1, 4)))
    coupling = bell_draw(seeds[1], (SLAVES, NS, 2, FW), (NS ** -0.25), 1.0546875, ((0, 32), (1, 4)))
    slave_diag = jnp.clip(jnp.exp(math.log(2.0) - 1.3862944 * jax.random.uniform(seeds[2], (SLAVES, NS), jnp.float32) ** shard_levels(seeds[2], (SLAVES, NS), ((0, 32), (1, 4)), -0.2, 0.2)), 0.5, 2.0)
    slave_masters_keys = jax.random.split(jax.random.fold_in(seeds[3], 1), SLAVES // SB_DEV)
    slave_masters_turns = jax.random.permutation(jax.random.fold_in(seeds[3], 3), SLAVES // SB_DEV)
    slave_masters = jax.vmap(lambda own, number: routed_block(jax.random.fold_in(seeds[3], 2), own, number, SB_DEV, MASTERS, 2, MOST, 2))(slave_masters_keys, slave_masters_turns).reshape((SLAVES, 2))
    return dict(stiffness=stiffness, coupling=coupling, slave_diag=slave_diag, slave_masters=slave_masters)


def slave_fill(operands):
    stiff, coup, diag = operands
    proj = (coup.astype(jnp.float32) / diag[:, None, None]).astype(jnp.bfloat16).reshape(NS, 2 * FW)
    applied = jnp.dot(stiff, proj, preferred_element_type=jnp.float32).astype(jnp.bfloat16)
    first = proj[:, :FW]
    second = proj[:, FW:]
    fill_aa = jnp.dot(first.T, applied[:, :FW], preferred_element_type=jnp.float32)
    fill_bb = jnp.dot(second.T, applied[:, FW:], preferred_element_type=jnp.float32)
    fill_ab = jnp.dot(first.T, applied[:, FW:], preferred_element_type=jnp.float32)
    return jnp.stack((fill_aa, fill_bb, fill_ab)).astype(jnp.bfloat16)


def reference(stiffness, coupling, slave_diag, slave_masters):
    fills = lax.map(slave_fill, (stiffness, coupling, slave_diag))
    cross_fill = fills[:, 2]
    masters = jnp.arange(MASTERS).astype(jnp.int32)
    onehot = (slave_masters[:, :, None] == masters[None, None, :]).astype(jnp.float32)
    grouped_hot = onehot.reshape(N_COL, SB_DEV, 2, MASTERS)
    grouped_fill = fills[:, :2].reshape(N_COL, SB_DEV, 2, FW, FW)

    def add_group(total, operands):
        hot, part = operands
        partial_sum = jnp.einsum("skm,skij->mij", hot, part.astype(jnp.float32)).astype(jnp.bfloat16)
        return total + partial_sum.astype(jnp.float32), None

    start_total = jnp.zeros((MASTERS, FW, FW), jnp.float32)
    total, unused = lax.scan(add_group, start_total, (grouped_hot, grouped_fill))
    return cross_fill, total.astype(jnp.bfloat16)
```

```python
import functools

import jax
import jax.numpy as jnp
from jax import lax
from jax.experimental import pallas as pl
from jax.experimental.pallas import tpu as pltpu
from jax.sharding import PartitionSpec as P

MESH = pl.DeviceIdType.MESH
F32 = jnp.float32
BF16 = jnp.bfloat16
ROWS = 4
NB = 5
QN = 256
NS = 1024
FW = 768
QF = FW // ROWS
HF = QF // 2
HC = FW // 2
NONE = 4 * NB


def kernel(
    stiff, coup, inv, table,
    cross, diag,
    kbuf, pbuf, cin, ploc, left, fills, terms, dense, got1, part, got2, last, idx_v, idx_s,
    k_send, k_recv, c_sem, p_send, p_recv, t_send, t_recv, x_send, x_recv,
    s1_send, s1_recv, s2_send, s2_recv, f_send, f_recv, i_sem, i_send, i_recv,
):
    r = lax.axis_index("row")
    c = lax.axis_index("col")
    core = lax.rem(c, 2)
    y = lax.rem(c // 2, 4)
    z = c // 8
    other = c + 1 - 2 * core
    target = 2 * core

    def at_y(v):
        return z * 8 + v * 2 + core

    def at_z(v):
        return v * 8 + y * 2 + core

    def wait(ref, sem):
        pltpu.make_async_copy(ref, ref, sem).wait()

    def remote(src, dst, send, recv, device):
        return pltpu.make_async_remote_copy(
            src_ref=src, dst_ref=dst, send_sem=send, recv_sem=recv, device_id=device, device_id_type=MESH
        )

    order = [4] + [lax.rem(r + d, ROWS) for d in (1, 2, 3, 0)]
    loads = [pltpu.make_async_copy(coup.at[b], cin.at[b], c_sem.at[i]) for i, b in enumerate(order)]
    for load in loads:
        load.start()

    barrier = pltpu.get_barrier_semaphore()
    partners = [(r, other)]
    for d in (1, 2, 3):
        row = lax.rem(r + d, ROWS)
        partners += [(row, c), (row, other), (r, at_y(lax.rem(y + d, 4))), (r, at_z(lax.rem(z + d, 4)))]
    for device in partners:
        pl.semaphore_signal(barrier, inc=1, device_id=device, device_id_type=MESH)
    pl.semaphore_wait(barrier, len(partners))

    mine = pl.ds(pl.multiple_of(r * QN, QN), QN)

    def k_copy(i, b, slot, row):
        return remote(stiff.at[b], kbuf.at[slot, mine], k_send.at[i], k_recv.at[slot, r], (row, c))

    def k_local(b, slot):
        return pltpu.make_async_copy(stiff.at[b], kbuf.at[slot, mine], k_recv.at[slot, r])

    def p_copy(i, b, slot, row, k):
        return remote(
            ploc.at[b, pl.ds(k * FW, FW)], pbuf.at[slot, pl.ds(k * FW, FW), mine],
            p_send.at[i, k], p_recv.at[slot, r, k], (row, c),
        )

    def p_local(b, slot, k):
        return pltpu.make_async_copy(
            ploc.at[b, pl.ds(k * FW, FW)], pbuf.at[slot, pl.ds(k * FW, FW), mine], p_recv.at[slot, r, k]
        )

    def send_block(i, remote_copy, local_copy):
        if i == 0:
            @pl.when(r == target)
            def _():
                local_copy(4, 0).start()

            @pl.when(r != target)
            def _():
                remote_copy(0, 4, 0, target).start()
        elif i < 4:
            remote_copy(i, order[i], 1, order[i]).start()
        else:
            local_copy(order[i], 1).start()

    for i in range(NB):
        send_block(i, k_copy, k_local)

    own_idx = pltpu.make_async_copy(table, idx_v.at[core], i_sem.at[0])
    own_idx.start()
    idx_copy = remote(table, idx_v.at[core], i_send, i_recv, (r, other))
    idx_copy.start()

    for i, b in enumerate(order):
        loads[i].wait()
        for k in range(2):
            raw = cin[b, :, k, :].astype(F32).T
            ploc[b, pl.ds(k * FW, FW), :] = (raw / inv[b]).astype(BF16)
            send_block(i, functools.partial(p_copy, k=k), functools.partial(p_local, k=k))

    terms[NONE] = jnp.zeros((HF, FW), BF16)
    own_idx.wait()
    idx_copy.wait()
    to_smem = pltpu.make_async_copy(idx_v, idx_s, i_sem.at[1])
    to_smem.start()
    to_smem.wait()

    def t_copies(slot, b, f, local=True):
        at = core * 2 * NB + b * 2 + f
        copies = []
        for dq in range(ROWS):
            for dh in range(2):
                q, h = lax.rem(r + dq, ROWS), lax.rem(core + dh, 2)
                src = fills.at[slot, f, pl.ds(pl.multiple_of(q * QF + h * HF, HF), HF)]
                if dq or dh:
                    copies.append(remote(
                        src, terms.at[at], t_send.at[slot, f, dq * 2 + dh], t_recv.at[at],
                        (q, c - core + h),
                    ))
                elif local:
                    copies.append(pltpu.make_async_copy(src, terms.at[at], t_recv.at[at]))
        return copies

    def x_copies(slot, b, local=True):
        copies = []
        for dq in range(ROWS):
            q = lax.rem(r + dq, ROWS)
            src = fills.at[slot, 2, pl.ds(pl.multiple_of(q * QF, QF), QF)]
            if dq:
                copies.append(remote(src, cross.at[b], x_send.at[slot, dq], x_recv.at[b], (q, c)))
            elif local:
                copies.append(pltpu.make_async_copy(src, cross.at[b], x_recv.at[b]))
        return copies

    def fill(slot, f, a, b):
        for n in range(3):
            out = lax.dot_general(
                left[a], pbuf[slot, pl.ds(b * FW + n * 256, 256), :],
                (((1,), (1,)), ((), ())), preferred_element_type=F32,
            )
            fills[slot, f, :, pl.ds(n * 256, 256)] = out.astype(BF16)

    def block(slot, unused):
        b = jnp.where(slot == 0, 4, r)
        for j in range(ROWS):
            wait(kbuf.at[slot, pl.ds(j * QN, QN)], k_recv.at[slot, j])
        for k in range(2):
            for j in range(ROWS):
                wait(pbuf.at[slot, pl.ds(k * FW, FW), pl.ds(j * QN, QN)], p_recv.at[slot, j, k])
            for n in range(4):
                out = jnp.dot(
                    pbuf[slot, pl.ds(k * FW, FW), :], kbuf[slot, :, pl.ds(n * 256, 256)],
                    preferred_element_type=F32,
                )
                left[k, :, pl.ds(n * 256, 256)] = out.astype(BF16)
            fill(slot, k, k, k)
            for copy in t_copies(slot, b, k):
                copy.start()
        fill(slot, 2, 0, 1)
        for copy in x_copies(slot, b):
            copy.start()
        return unused

    lax.fori_loop(jnp.where(r == target, 0, 1), 2, block, 0)

    for at in range(NONE):
        wait(terms.at[at], t_recv.at[at])

    def sum_terms(half, lead, cols):
        def one(j, unused):
            o, h = j // 2, lax.rem(j, 2)
            zz, yy = (o, lead) if half == 0 else (lead, o)
            m = zz * 8 + yy * 2 + h
            total = terms[idx_s[0, 0, m], :, cols].astype(F32) + terms[idx_s[0, 1, m], :, cols].astype(F32)
            total += terms[idx_s[1, 0, m], :, cols].astype(F32) + terms[idx_s[1, 1, m], :, cols].astype(F32)
            dense[half, lead, o, h] = total.astype(BF16)
            return unused

        lax.fori_loop(0, 8, one, 0)

    place = (y, z)
    whom = (at_y, at_z)
    columns = (pl.ds(0, HC), pl.ds(HC, HC))
    first = [[None] * 4, [None] * 4]
    for d in (2, 1, 3, 0):
        for half in range(2):
            lead = lax.rem(place[half] + d, 4)
            sum_terms(half, lead, columns[half])
            if d:
                copy = remote(
                    dense.at[half, lead], got1.at[half, d - 1],
                    s1_send.at[half, d - 1], s1_recv.at[half, d - 1], (r, whom[half](lead)),
                )
                copy.start()
                first[half][d] = copy

    second = [[None] * 4, [None] * 4]
    for half in range(2):
        for d in (1, 2, 3):
            first[half][d].wait_recv()
        for d in (2, 1, 3, 0):
            o = lax.rem(place[1 - half] + d, 4)
            total = dense[half, place[half], o].astype(F32)
            for e in range(3):
                total += got1[half, e, o].astype(F32)
            part[half, o] = total.astype(BF16)
            if d:
                copy = remote(
                    part.at[half, o], got2.at[half, d - 1],
                    s2_send.at[half, d - 1], s2_recv.at[half, d - 1], (r, whom[1 - half](o)),
                )
                copy.start()
                second[half][d] = copy

    for half in range(2):
        for d in (1, 2, 3):
            second[half][d].wait_recv()
        total = part[half, place[1 - half]].astype(F32)
        for e in range(3):
            total += got2[half, e].astype(F32)
        last[:, :, columns[half]] = total.astype(BF16)

    own_rows = pl.ds(pl.multiple_of(core * HF, HF), HF)
    keep = pltpu.make_async_copy(last.at[core], diag.at[0, own_rows], f_recv.at[core])
    keep.start()
    give = remote(last.at[1 - core], diag.at[0, own_rows], f_send, f_recv.at[core], (r, other))
    give.start()

    for b in range(NB):
        wait(cross.at[b], x_recv.at[b])
    for h in range(2):
        wait(diag.at[0, pl.ds(h * HF, HF)], f_recv.at[h])
    give.wait_send()
    for half in range(2):
        for d in (1, 2, 3):
            first[half][d].wait_send()
            second[half][d].wait_send()

    @pl.when(r != target)
    def _():
        k_copy(0, 4, 0, target).wait_send()
        for k in range(2):
            p_copy(0, 4, 0, target, k).wait_send()

    for i in (1, 2, 3):
        k_copy(i, order[i], 1, order[i]).wait_send()
        for k in range(2):
            p_copy(i, order[i], 1, order[i], k).wait_send()

    def drain(slot, unused):
        b = jnp.where(slot == 0, 4, r)
        for f in range(2):
            for copy in t_copies(slot, b, f, False):
                copy.wait_send()
        for copy in x_copies(slot, b, False):
            copy.wait_send()
        return unused

    lax.fori_loop(jnp.where(r == target, 0, 1), 2, drain, 0)


def per_device(stiffness, coupling, slave_diag, slave_masters):
    core = lax.rem(lax.axis_index("col"), 2)
    refs = jnp.arange(2 * NB, dtype=jnp.int32)
    hit = slave_masters.reshape(1, 2 * NB) == jnp.arange(128, dtype=jnp.int32)[:, None]
    low = jnp.min(jnp.where(hit, refs, 2 * NB), axis=1)
    high = jnp.max(jnp.where(hit, refs, -1), axis=1)
    base = core * 2 * NB
    table = jnp.stack((
        jnp.where(high >= 0, low + base, NONE),
        jnp.where(high > low, high + base, NONE),
    ))
    table = jnp.pad(table, ((0, 6), (0, 0))).astype(jnp.int32)
    any_space = pl.BlockSpec(memory_space=pl.ANY)
    vmem = pl.BlockSpec(memory_space=pltpu.VMEM)
    dma = pltpu.SemaphoreType.DMA
    flops = 2 * NB * (2 * NS * NS * FW + 3 * FW * FW * NS) // 4
    return pl.pallas_call(
        kernel,
        out_shape=(
            jax.ShapeDtypeStruct((NB, QF, FW), BF16),
            jax.ShapeDtypeStruct((1, QF, FW), BF16),
        ),
        in_specs=[any_space, any_space, vmem, vmem],
        out_specs=(any_space, any_space),
        scratch_shapes=[
            pltpu.VMEM((2, NS, NS), BF16),
            pltpu.VMEM((2, 2 * FW, NS), BF16),
            pltpu.VMEM((NB, QN, 2, FW), BF16),
            pltpu.VMEM((NB, 2 * FW, QN), BF16),
            pltpu.VMEM((2, FW, NS), BF16),
            pltpu.VMEM((2, 3, FW, FW), BF16),
            pltpu.VMEM((NONE + 1, HF, FW), BF16),
            pltpu.VMEM((2, 4, 4, 2, HF, HC), BF16),
            pltpu.VMEM((2, 3, 4, 2, HF, HC), BF16),
            pltpu.VMEM((2, 4, 2, HF, HC), BF16),
            pltpu.VMEM((2, 3, 2, HF, HC), BF16),
            pltpu.VMEM((2, HF, FW), BF16),
            pltpu.VMEM((2, 8, 128), jnp.int32),
            pltpu.SMEM((2, 8, 128), jnp.int32),
            dma((NB,)), dma((2, ROWS)), dma((NB,)), dma((NB, 2)), dma((2, ROWS, 2)),
            dma((2, 2, 8)), dma((NONE,)), dma((2, ROWS)), dma((NB,)),
            dma((2, 3)), dma((2, 3)), dma((2, 3)), dma((2, 3)), dma, dma((2,)), dma((2,)), dma, dma,
        ],
        compiler_params=pltpu.CompilerParams(
            collective_id=0, has_side_effects=True, vmem_limit_bytes=58 * 2**20
        ),
        cost_estimate=pl.CostEstimate(flops=flops, bytes_accessed=9 * 2**20, transcendentals=0),
        name="condense",
    )(stiffness, coupling, slave_diag.reshape(NB, 1, QN), table)


def solution(mesh):
    return jax.shard_map(
        per_device,
        mesh=mesh,
        in_specs=(
            P("col", "row", None),
            P("col", "row", None, None),
            P("col", "row"),
            P("col", None),
        ),
        out_specs=(P("col", "row", None), P("col", "row", None)),
        check_vma=False,
    )
```

```python
import functools

import jax
import jax.numpy as jnp
from jax import lax
from jax.experimental import pallas as pl
from jax.experimental.pallas import tpu as pltpu
from jax.sharding import PartitionSpec as P

MESH = pl.DeviceIdType.MESH
F32 = jnp.float32
BF16 = jnp.bfloat16
ROWS = 4
NB = 5
QN = 256
NS = 1024
FW = 768
QF = FW // ROWS
HF = QF // 2
HC = FW // 2
NONE = 4 * NB
CH = 3
CR = HF // CH


def kernel(
    stiff, coup, scale, masters,
    cross, diag,
    kbuf, pbuf, cin, ploc, left, fills, terms0, terms1, terms2, dense, got1, part, got2, last, own_table, idx_v, idx_s,
    k_send, k_recv, c_sem, p_send, p_recv, t_send, t_recv, x_send, x_recv,
    s1_send, s1_recv, s2_send, s2_recv, f_send, f_recv, i_sem, i_send, i_recv,
):
    r = lax.axis_index("row")
    c = lax.axis_index("col")
    terms = (terms0, terms1, terms2)
    core = lax.rem(c, 2)
    y = lax.rem(c // 2, 4)
    z = c // 8
    other = c + 1 - 2 * core
    target = 2 * core

    def at_y(v):
        return z * 8 + v * 2 + core

    def at_z(v):
        return v * 8 + y * 2 + core

    def wait(ref, sem):
        pltpu.make_async_copy(ref, ref, sem).wait()

    def remote(src, dst, send, recv, device):
        return pltpu.make_async_remote_copy(
            src_ref=src, dst_ref=dst, send_sem=send, recv_sem=recv, device_id=device, device_id_type=MESH
        )

    order = [4] + [lax.rem(r + d, ROWS) for d in (1, 2, 3, 0)]
    loads = [pltpu.make_async_copy(coup.at[b], cin.at[b], c_sem.at[i]) for i, b in enumerate(order)]
    for load in loads:
        load.start()

    lane = lax.broadcasted_iota(jnp.int32, (8, 128), 1)
    low, high = jnp.full((8, 128), NONE, jnp.int32), jnp.full((8, 128), -1, jnp.int32)
    for e in range(2 * NB):
        hit = lane == jnp.broadcast_to(masters[pl.ds(e % 2, 1), pl.ds(e // 2, 1)], (8, 128))
        low = jnp.minimum(low, jnp.where(hit, core * 2 * NB + e, NONE))
        high = jnp.maximum(high, jnp.where(hit, core * 2 * NB + e, -1))
    own_table[0] = low
    own_table[1] = jnp.where(high > low, high, NONE)

    barrier = pltpu.get_barrier_semaphore()
    partners = [(r, other)]
    for d in (1, 2, 3):
        row = lax.rem(r + d, ROWS)
        partners += [(row, c), (row, other), (r, at_y(lax.rem(y + d, 4))), (r, at_z(lax.rem(z + d, 4)))]
    for device in partners:
        pl.semaphore_signal(barrier, inc=1, device_id=device, device_id_type=MESH)
    pl.semaphore_wait(barrier, len(partners))

    mine = pl.ds(pl.multiple_of(r * QN, QN), QN)

    def k_copy(i, b, slot, row):
        return remote(stiff.at[b], kbuf.at[slot, mine], k_send.at[i], k_recv.at[slot, r], (row, c))

    def k_local(b, slot):
        return pltpu.make_async_copy(stiff.at[b], kbuf.at[slot, mine], k_recv.at[slot, r])

    def p_copy(i, b, slot, row, k):
        return remote(
            ploc.at[b, pl.ds(k * FW, FW)], pbuf.at[slot, pl.ds(k * FW, FW), mine],
            p_send.at[i, k], p_recv.at[slot, r, k], (row, c),
        )

    def p_local(b, slot, k):
        return pltpu.make_async_copy(
            ploc.at[b, pl.ds(k * FW, FW)], pbuf.at[slot, pl.ds(k * FW, FW), mine], p_recv.at[slot, r, k]
        )

    def send_block(i, remote_copy, local_copy):
        if i == 0:
            @pl.when(r == target)
            def _():
                local_copy(4, 0).start()

            @pl.when(r != target)
            def _():
                remote_copy(0, 4, 0, target).start()
        elif i < 4:
            remote_copy(i, order[i], 1, order[i]).start()
        else:
            local_copy(order[i], 1).start()

    for i in range(NB):
        send_block(i, k_copy, k_local)

    own_idx = pltpu.make_async_copy(own_table, idx_v.at[core], i_sem.at[0])
    own_idx.start()
    idx_copy = remote(own_table, idx_v.at[core], i_send, i_recv, (r, other))
    idx_copy.start()

    for i, k in [(0, 0), (0, 1)] + [(i, k) for k in range(2) for i in range(1, NB)]:
        b = order[i]
        if k == 0:
            loads[i].wait()
        raw = cin[b, :, k, :].astype(F32).T
        ploc[b, pl.ds(k * FW, FW), :] = (raw / scale[pl.ds(b, 1), :]).astype(BF16)
        send_block(i, functools.partial(p_copy, k=k), functools.partial(p_local, k=k))

    for chunk in terms:
        chunk[NONE] = jnp.zeros((CR, FW), BF16)
    own_idx.wait()
    idx_copy.wait()
    to_smem = pltpu.make_async_copy(idx_v, idx_s, i_sem.at[1])
    to_smem.start()
    to_smem.wait()

    def t_copies(slot, b, f, j, local=True):
        at = core * 2 * NB + b * 2 + f
        copies = []
        for dq in range(ROWS):
            for dh in range(2):
                q, h = lax.rem(r + dq, ROWS), lax.rem(core + dh, 2)
                src = fills.at[slot, f, pl.ds(pl.multiple_of(q * QF + h * HF + j * CR, CR), CR)]
                dst = terms[j].at[at]
                if dq or dh:
                    copies.append(remote(
                        src, dst, t_send.at[slot, f, j, dq * 2 + dh], t_recv.at[j, at], (q, c - core + h)
                    ))
                elif local:
                    copies.append(pltpu.make_async_copy(src, dst, t_recv.at[j, at]))
        return copies

    def x_copies(slot, b, local=True):
        copies = []
        for dq in range(ROWS):
            q = lax.rem(r + dq, ROWS)
            src = fills.at[slot, 2, pl.ds(pl.multiple_of(q * QF, QF), QF)]
            if dq:
                copies.append(remote(src, cross.at[b], x_send.at[slot, dq], x_recv.at[b], (q, c)))
            elif local:
                copies.append(pltpu.make_async_copy(src, cross.at[b], x_recv.at[b]))
        return copies

    def fill(slot, f, a, b):
        for n in range(3):
            out = lax.dot_general(
                left[a], pbuf[slot, pl.ds(b * FW + n * 256, 256), :],
                (((1,), (1,)), ((), ())), preferred_element_type=F32,
            )
            fills[slot, f, :, pl.ds(n * 256, 256)] = out.astype(BF16)

    def multiply(slot, k):
        for n in range(4):
            out = jnp.dot(
                pbuf[slot, pl.ds(k * FW, FW), :], kbuf[slot, :, pl.ds(n * 256, 256)],
                preferred_element_type=F32,
            )
            left[k, :, pl.ds(n * 256, 256)] = out.astype(BF16)

    def block(slot, unused):
        b = jnp.where(slot == 0, 4, r)

        def p_wait(k):
            for j in range(ROWS):
                wait(pbuf.at[slot, pl.ds(k * FW, FW), pl.ds(j * QN, QN)], p_recv.at[slot, j, k])

        def t_start(f, j):
            for copy in t_copies(slot, b, f, j):
                copy.start()

        for j in range(ROWS):
            wait(kbuf.at[slot, pl.ds(j * QN, QN)], k_recv.at[slot, j])
        p_wait(0)
        multiply(slot, 0)
        fill(slot, 0, 0, 0)
        p_wait(1)
        t_start(0, 0)
        t_start(0, 1)
        multiply(slot, 1)
        fill(slot, 1, 1, 1)
        t_start(1, 0)
        t_start(1, 1)
        t_start(0, 2)
        t_start(1, 2)
        fill(slot, 2, 0, 1)
        for copy in x_copies(slot, b):
            copy.start()
        return unused

    lax.fori_loop(jnp.where(r == target, 0, 1), 2, block, 0)

    place = (y, z)
    whom = (at_y, at_z)
    columns = (pl.ds(0, HC), pl.ds(HC, HC))

    def sum_terms(j, half, lead):
        chunk, cols = terms[j], columns[half]

        def one(n, unused):
            o, h = n // 2, lax.rem(n, 2)
            zz, yy = (o, lead) if half == 0 else (lead, o)
            m = zz * 8 + yy * 2 + h
            total = chunk[idx_s[0, 0, 0, m], :, cols].astype(F32) + chunk[idx_s[0, 1, 0, m], :, cols].astype(F32)
            total += chunk[idx_s[1, 0, 0, m], :, cols].astype(F32) + chunk[idx_s[1, 1, 0, m], :, cols].astype(F32)
            dense[j, half, lead, o, h] = total.astype(BF16)
            return unused

        lax.fori_loop(0, 8, one, 0)

    def first_copy(j, half, d):
        lead = lax.rem(place[half] + d, 4)
        return remote(
            dense.at[j, half, lead], got1.at[j, half, d - 1],
            s1_send.at[j, half, d - 1], s1_recv.at[j, half, d - 1], (r, whom[half](lead)),
        )

    def second_copy(j, half, d):
        o = lax.rem(place[1 - half] + d, 4)
        return remote(
            part.at[j, half, o], got2.at[j, half, d - 1],
            s2_send.at[j, half, d - 1], s2_recv.at[j, half, d - 1], (r, whom[1 - half](o)),
        )

    def stage0(j):
        for at in range(NONE):
            wait(terms[j].at[at], t_recv.at[j, at])
        for d in (2, 1, 3, 0):
            for half in range(2):
                sum_terms(j, half, lax.rem(place[half] + d, 4))
                if d:
                    first_copy(j, half, d).start()

    def stage1(j):
        for half in range(2):
            for d in (1, 2, 3):
                first_copy(j, half, d).wait_recv()
            for d in (2, 1, 3, 0):
                o = lax.rem(place[1 - half] + d, 4)
                total = dense[j, half, place[half], o].astype(F32)
                for e in range(3):
                    total += got1[j, half, e, o].astype(F32)
                part[j, half, o] = total.astype(BF16)
                if d:
                    second_copy(j, half, d).start()

    def out_rows(j, h):
        return diag.at[0, pl.ds(pl.multiple_of(h * HF + j * CR, CR), CR)]

    def give(j):
        return remote(
            last.at[1 - core, pl.ds(j * CR, CR)], out_rows(j, core),
            f_send.at[j], f_recv.at[j, core], (r, other),
        )

    def stage2(j):
        rows = pl.ds(j * CR, CR)
        for half in range(2):
            for d in (1, 2, 3):
                second_copy(j, half, d).wait_recv()
            total = part[j, half, place[1 - half]].astype(F32)
            for e in range(3):
                total += got2[j, half, e].astype(F32)
            last[:, rows, columns[half]] = total.astype(BF16)
        pltpu.make_async_copy(last.at[core, rows], out_rows(j, core), f_recv.at[j, core]).start()
        give(j).start()

    stage0(0)
    stage0(1)
    stage1(0)
    stage0(2)
    stage1(1)
    stage2(0)
    stage1(2)
    stage2(1)
    stage2(2)

    for b in range(NB):
        wait(cross.at[b], x_recv.at[b])
    for j in range(CH):
        for h in range(2):
            wait(out_rows(j, h), f_recv.at[j, h])
        give(j).wait_send()
        for half in range(2):
            for d in (1, 2, 3):
                first_copy(j, half, d).wait_send()
                second_copy(j, half, d).wait_send()

    @pl.when(r != target)
    def _():
        k_copy(0, 4, 0, target).wait_send()
        for k in range(2):
            p_copy(0, 4, 0, target, k).wait_send()

    for i in (1, 2, 3):
        k_copy(i, order[i], 1, order[i]).wait_send()
        for k in range(2):
            p_copy(i, order[i], 1, order[i], k).wait_send()

    def drain(slot, unused):
        b = jnp.where(slot == 0, 4, r)
        for f in range(2):
            for j in range(CH):
                for copy in t_copies(slot, b, f, j, False):
                    copy.wait_send()
        for copy in x_copies(slot, b, False):
            copy.wait_send()
        return unused

    lax.fori_loop(jnp.where(r == target, 0, 1), 2, drain, 0)


def per_device(stiffness, coupling, slave_diag, slave_masters):
    any_space = pl.BlockSpec(memory_space=pl.ANY)
    vmem = pl.BlockSpec(memory_space=pltpu.VMEM)
    dma = pltpu.SemaphoreType.DMA
    flops = 2 * NB * (2 * NS * NS * FW + 3 * FW * FW * NS) // 4
    return pl.pallas_call(
        kernel,
        out_shape=(
            jax.ShapeDtypeStruct((NB, QF, FW), BF16),
            jax.ShapeDtypeStruct((1, QF, FW), BF16),
        ),
        in_specs=[any_space, any_space, vmem, vmem],
        out_specs=(any_space, any_space),
        scratch_shapes=[
            pltpu.VMEM((2, NS, NS), BF16),
            pltpu.VMEM((2, 2 * FW, NS), BF16),
            pltpu.VMEM((NB, QN, 2, FW), BF16),
            pltpu.VMEM((NB, 2 * FW, QN), BF16),
            pltpu.VMEM((2, FW, NS), BF16),
            pltpu.VMEM((2, 3, FW, FW), BF16),
            *[pltpu.VMEM((NONE + 1, CR, FW), BF16)] * CH,
            pltpu.VMEM((CH, 2, 4, 4, 2, CR, HC), BF16),
            pltpu.VMEM((CH, 2, 3, 4, 2, CR, HC), BF16),
            pltpu.VMEM((CH, 2, 4, 2, CR, HC), BF16),
            pltpu.VMEM((CH, 2, 3, 2, CR, HC), BF16),
            pltpu.VMEM((2, HF, FW), BF16),
            pltpu.VMEM((2, 8, 128), jnp.int32),
            pltpu.VMEM((2, 2, 8, 128), jnp.int32),
            pltpu.SMEM((2, 2, 8, 128), jnp.int32),
            dma((NB,)), dma((2, ROWS)), dma((NB,)), dma((NB, 2)), dma((2, ROWS, 2)),
            dma((2, 2, CH, 8)), dma((CH, NONE)), dma((2, ROWS)), dma((NB,)),
            dma((CH, 2, 3)), dma((CH, 2, 3)), dma((CH, 2, 3)), dma((CH, 2, 3)),
            dma((CH,)), dma((CH, 2)), dma((2,)), dma, dma,
        ],
        compiler_params=pltpu.CompilerParams(
            collective_id=0, has_side_effects=True, vmem_limit_bytes=58 * 2**20
        ),
        cost_estimate=pl.CostEstimate(flops=flops, bytes_accessed=9 * 2**20, transcendentals=0),
        name="condense",
    )(stiffness, coupling, slave_diag, slave_masters.T)


def solution(mesh):
    return jax.shard_map(
        per_device,
        mesh=mesh,
        in_specs=(
            P("col", "row", None),
            P("col", "row", None, None),
            P("col", "row"),
            P("col", None),
        ),
        out_specs=(P("col", "row", None), P("col", "row", None)),
        check_vma=False,
    )
```

```python
import functools

import jax
import jax.numpy as jnp
from jax import lax
from jax.experimental import pallas as pl
from jax.experimental.pallas import tpu as pltpu
from jax.sharding import PartitionSpec as P

MESH = pl.DeviceIdType.MESH
F32 = jnp.float32
BF16 = jnp.bfloat16
ROWS = 4
NB = 5
QN = 256
NS = 1024
FW = 768
QF = FW // ROWS
HF = QF // 2
HC = FW // 2
NONE = 4 * NB
CH = 3
CR = HF // CH


def kernel(
    stiff, coup, scale, masters,
    cross, diag,
    kbuf, pbuf, cin, ploc, relay, left, fills, dense, got1, part, got2, last, own_table, idx_v, idx_s,
    k_send, k_recv, c_sem, p_send, p_recv, r_send, r_recv, t_send, t_recv, x_send, x_recv,
    s1_send, s1_recv, s2_send, s2_recv, f_sem, i_sem, i_send, i_recv, ready, *terms,
):
    r = lax.axis_index("row")
    c = lax.axis_index("col")
    core = lax.rem(c, 2)
    y = lax.rem(c // 2, 4)
    z = c // 8
    other = c + 1 - 2 * core
    target = 2 * core
    through = target + 1
    far = lax.rem(target + 2, ROWS)

    def at_y(v, h=core):
        return z * 8 + v * 2 + h

    def at_z(v, h=core):
        return v * 8 + y * 2 + h

    def wait(ref, sem):
        pltpu.make_async_copy(ref, ref, sem).wait()

    def remote(src, dst, send, recv, device):
        return pltpu.make_async_remote_copy(
            src_ref=src, dst_ref=dst, send_sem=send, recv_sem=recv, device_id=device, device_id_type=MESH
        )

    order = [4] + [lax.rem(r + d, ROWS) for d in (1, 2, 3, 0)]
    loads = [pltpu.make_async_copy(coup.at[b], cin.at[b], c_sem.at[i]) for i, b in enumerate(order)]
    for load in loads:
        load.start()

    lane = lax.broadcasted_iota(jnp.int32, (8, 128), 1)
    low, high = jnp.full((8, 128), NONE, jnp.int32), jnp.full((8, 128), -1, jnp.int32)
    for e in range(2 * NB):
        hit = lane == jnp.broadcast_to(masters[pl.ds(e % 2, 1), pl.ds(e // 2, 1)], (8, 128))
        low = jnp.minimum(low, jnp.where(hit, core * 2 * NB + e, NONE))
        high = jnp.maximum(high, jnp.where(hit, core * 2 * NB + e, -1))
    own_table[0] = low
    own_table[1] = jnp.where(high > low, high, NONE)

    barrier = pltpu.get_barrier_semaphore()
    partners = [(r, other)]
    for d in (1, 2, 3):
        row = lax.rem(r + d, ROWS)
        partners += [(row, c), (row, other)]
        for h in (core, 1 - core):
            partners += [(r, at_y(lax.rem(y + d, 4), h)), (r, at_z(lax.rem(z + d, 4), h))]
    for device in partners:
        pl.semaphore_signal(barrier, inc=1, device_id=device, device_id_type=MESH)
    pl.semaphore_wait(barrier, len(partners))

    mine = pl.ds(pl.multiple_of(r * QN, QN), QN)

    def k_copy(i, b, slot, row):
        return remote(stiff.at[b], kbuf.at[slot, mine], k_send.at[i], k_recv.at[slot, r], (row, c))

    def k_local(b, slot):
        return pltpu.make_async_copy(stiff.at[b], kbuf.at[slot, mine], k_recv.at[slot, r])

    def p_copy(i, b, slot, row, k):
        return remote(
            ploc.at[b, pl.ds(k * FW, FW)], pbuf.at[slot, pl.ds(k * FW, FW), mine],
            p_send.at[i, k], p_recv.at[slot, r, k], (row, c),
        )

    def p_aside(k):
        return remote(
            ploc.at[4, pl.ds(k * FW, FW)], relay.at[pl.ds(k * FW, FW)],
            p_send.at[0, k], r_recv.at[k], (through, c),
        )

    def p_forward(k):
        return remote(
            relay.at[pl.ds(k * FW, FW)],
            pbuf.at[0, pl.ds(k * FW, FW), pl.ds(pl.multiple_of(far * QN, QN), QN)],
            r_send.at[k], p_recv.at[0, far, k], (target, c),
        )

    def p_local(b, slot, k):
        return pltpu.make_async_copy(
            ploc.at[b, pl.ds(k * FW, FW)], pbuf.at[slot, pl.ds(k * FW, FW), mine], p_recv.at[slot, r, k]
        )

    def send_block(i, remote_copy, local_copy, aside=None):
        if i == 0:
            @pl.when(r == target)
            def _():
                local_copy(4, 0).start()

            @pl.when((r != target) & (r != far if aside else True))
            def _():
                remote_copy(0, 4, 0, target).start()

            if aside:
                @pl.when(r == far)
                def _():
                    aside().start()
        elif i == 3:
            @pl.when(r != through)
            def _():
                remote_copy(i, order[i], 1, order[i]).start()
        elif i < 4:
            remote_copy(i, order[i], 1, order[i]).start()
        else:
            local_copy(order[i], 1).start()

    send_block(0, k_copy, k_local)

    def project(i, k):
        b = order[i]
        if k == 0:
            loads[i].wait()
        raw = cin[b, :, k, :].astype(F32).T
        ploc[b, pl.ds(k * FW, FW), :] = (raw / scale[pl.ds(b, 1), :]).astype(BF16)
        send_block(
            i, functools.partial(p_copy, k=k), functools.partial(p_local, k=k), functools.partial(p_aside, k)
        )

    project(0, 0)
    project(0, 1)
    for i in range(1, NB):
        send_block(i, k_copy, k_local)
    for k in range(2):
        for i in range(1, NB):
            project(i, k)

    own_idx = pltpu.make_async_copy(own_table, idx_v.at[core], i_sem.at[0])
    own_idx.start()
    idx_copy = remote(own_table, idx_v.at[core], i_send, i_recv, (r, other))
    idx_copy.start()

    for chunk in terms:
        chunk[NONE] = jnp.zeros((CR, FW), BF16)
    own_idx.wait()
    idx_copy.wait()
    to_smem = pltpu.make_async_copy(idx_v, idx_s, i_sem.at[1])
    to_smem.start()
    to_smem.wait()

    @pl.when(r == through)
    def _():
        for k in range(2):
            wait(relay.at[pl.ds(k * FW, FW)], r_recv.at[k])
            p_forward(k).start()
        k_copy(3, order[3], 1, order[3]).start()
        for k in range(2):
            p_copy(3, order[3], 1, order[3], k).start()

    def t_copies(slot, b, f, j, local=True):
        at = core * 2 * NB + b * 2 + f
        copies = []
        for dq in range(ROWS):
            for dh in range(2):
                q, h = lax.rem(r + dq, ROWS), lax.rem(core + dh, 2)
                src = fills.at[slot, f, pl.ds(pl.multiple_of(q * QF + h * HF + j * CR, CR), CR)]
                dst = terms[j].at[at]
                if dq or dh:
                    copies.append(remote(
                        src, dst, t_send.at[slot, f, j, dq * 2 + dh], t_recv.at[j, at], (q, c - core + h)
                    ))
                elif local:
                    copies.append(pltpu.make_async_copy(src, dst, t_recv.at[j, at]))
        return copies

    def x_copies(slot, b, local=True):
        copies = []
        for dq in range(ROWS):
            q = lax.rem(r + dq, ROWS)
            src = fills.at[slot, 2, pl.ds(pl.multiple_of(q * QF, QF), QF)]
            if dq:
                copies.append(remote(src, cross.at[b], x_send.at[slot, dq], x_recv.at[b], (q, c)))
            elif local:
                copies.append(pltpu.make_async_copy(src, cross.at[b], x_recv.at[b]))
        return copies

    def fill(slot, f, a, b):
        for n in range(3):
            out = lax.dot_general(
                left[a], pbuf[slot, pl.ds(b * FW + n * 256, 256), :],
                (((1,), (1,)), ((), ())), preferred_element_type=F32,
            )
            fills[slot, f, :, pl.ds(n * 256, 256)] = out.astype(BF16)

    def multiply(slot, k):
        for n in range(4):
            out = jnp.dot(
                pbuf[slot, pl.ds(k * FW, FW), :], kbuf[slot, :, pl.ds(n * 256, 256)],
                preferred_element_type=F32,
            )
            left[k, :, pl.ds(n * 256, 256)] = out.astype(BF16)

    def block(slot, unused):
        b = jnp.where(slot == 0, 4, r)

        def p_wait(k):
            for j in range(ROWS):
                wait(pbuf.at[slot, pl.ds(k * FW, FW), pl.ds(j * QN, QN)], p_recv.at[slot, j, k])

        def t_start(f, j):
            for copy in t_copies(slot, b, f, j):
                copy.start()

        def k_wait():
            for j in range(ROWS):
                wait(kbuf.at[slot, pl.ds(j * QN, QN)], k_recv.at[slot, j])

        k_wait()
        p_wait(0)
        multiply(slot, 0)
        fill(slot, 0, 0, 0)
        p_wait(1)

        @pl.when(owner & (slot == 1))
        def _():
            for device in ring:
                pl.semaphore_signal(ready, inc=1, device_id=device, device_id_type=MESH)
            t_start(0, 0)

        multiply(slot, 1)
        fill(slot, 1, 1, 1)

        @pl.when(jnp.logical_not(owner))
        def _():
            fill(slot, 2, 0, 1)
            pl.semaphore_wait(ready, 2)

        @pl.when(jnp.logical_not(owner & (slot == 1)))
        def _():
            t_start(0, 0)

        t_start(1, 0)
        for j in range(1, CH):
            for f in range(2):
                t_start(f, j)

        @pl.when(owner)
        def _():
            fill(slot, 2, 0, 1)

        return unused

    owner = r == target
    def k_drain():
        @pl.when(r != target)
        def _():
            k_copy(0, 4, 0, target).wait_send()

        @pl.when((r != target) & (r != far))
        def _():
            for k in range(2):
                p_copy(0, 4, 0, target, k).wait_send()

        @pl.when(r == far)
        def _():
            for k in range(2):
                p_aside(k).wait_send()

        @pl.when(r == through)
        def _():
            for k in range(2):
                p_forward(k).wait_send()

        for i in (1, 2, 3):
            k_copy(i, order[i], 1, order[i]).wait_send()
            for k in range(2):
                p_copy(i, order[i], 1, order[i], k).wait_send()

    def t_drain(j):
        def one(slot, unused):
            for f in range(2):
                for copy in t_copies(slot, jnp.where(slot == 0, 4, r), f, j, False):
                    copy.wait_send()
            return unused

        lax.fori_loop(first_slot, 2, one, 0)

    first_slot = jnp.where(owner, 0, 1)
    ring = [(r, other)] + [(lax.rem(r + d, ROWS), col) for d in (1, 2, 3) for col in (c, other)]
    lax.fori_loop(first_slot, 2, block, 0)
    for copy in x_copies(1, r):
        copy.start()

    @pl.when(r == target)
    def _():
        for copy in x_copies(0, 4):
            copy.start()
        pl.semaphore_wait(ready, 1)

    k_drain()


    place = (y, z)
    whom = (at_y, at_z)
    columns = (pl.ds(0, HC), pl.ds(HC, HC))

    def sum_terms(j, half, lead):
        chunk, cols = terms[j], columns[half]

        def one(n, unused):
            o, h = n // 2, lax.rem(n, 2)
            zz, yy = (o, lead) if half == 0 else (lead, o)
            m = zz * 8 + yy * 2 + h
            total = chunk[idx_s[0, 0, 0, m], :, cols].astype(F32) + chunk[idx_s[0, 1, 0, m], :, cols].astype(F32)
            total += chunk[idx_s[1, 0, 0, m], :, cols].astype(F32) + chunk[idx_s[1, 1, 0, m], :, cols].astype(F32)
            dense[j, half, lead, o, h] = total.astype(BF16)
            return unused

        lax.fori_loop(0, 8, one, 0)

    def first_copy(j, half, d):
        lead = lax.rem(place[half] + d, 4)
        return remote(
            dense.at[j, half, lead], got1.at[j, half, d - 1],
            s1_send.at[j, half, d - 1], s1_recv.at[j, half, d - 1], (r, whom[half](lead)),
        )

    def second_copies(j, half, d):
        o = lax.rem(place[1 - half] + d, 4)
        return [
            remote(
                part.at[j, half, o, h], got2.at[j, half, d, core],
                s2_send.at[j, half, d, e], s2_recv.at[j, half, d, core], (r, whom[1 - half](o, h)),
            )
            for e, h in ((0, core), (1, 1 - core)) if d or e
        ]

    def t_wait(j):
        for at in range(NONE):
            wait(terms[j].at[at], t_recv.at[j, at])

    def first_wait(j, half):
        for d in (1, 2, 3):
            first_copy(j, half, d).wait_recv()

    def second_wait(j, half):
        for d in range(4):
            for h in (1 - core, core) if d else (1 - core,):
                wait(got2.at[j, half, d, h], s2_recv.at[j, half, d, h])

    def stage0(j):
        t_wait(j)
        for d in (2, 1, 3, 0):
            for half in range(2):
                sum_terms(j, half, lax.rem(place[half] + d, 4))
                if d:
                    first_copy(j, half, d).start()

    def stage1(j):
        t_drain(j)
        for half in range(2):
            first_wait(j, half)
            for d in (2, 1, 3, 0):
                o = lax.rem(place[1 - half] + d, 4)
                total = dense[j, half, place[half], o].astype(F32)
                for e in range(3):
                    total += got1[j, half, e, o].astype(F32)
                part[j, half, o] = total.astype(BF16)
                for copy in second_copies(j, half, d):
                    copy.start()
            got2[j, half, 0, core] = part[j, half, place[1 - half], core]

    def out_copy(j, h):
        rows = pl.ds(h * HF + j * CR, CR)
        return pltpu.make_async_copy(last.at[rows], diag.at[0, rows], f_sem.at[j, h])

    def stage2(j):
        for half in range(2):
            for d in (1, 2, 3):
                first_copy(j, half, d).wait_send()
            if j:
                for d in range(4):
                    for copy in second_copies(j - 1, half, d):
                        copy.wait_send()
        for half in range(2):
            second_wait(j, half)
            total = got2[j, half, 0].astype(F32)
            for d in (1, 2, 3):
                total += got2[j, half, d].astype(F32)
            total = total.astype(BF16)
            for h in range(2):
                last[pl.ds(h * HF + j * CR, CR), columns[half]] = total[h]
        for h in range(2):
            out_copy(j, h).start()

    stage0(0)
    stage0(1)
    stage1(0)
    for j in range(2, CH):
        stage0(j)
        stage1(j - 1)
        stage2(j - 2)
    stage1(CH - 1)
    stage2(CH - 2)
    stage2(CH - 1)

    def x_wait():
        for b in range(NB):
            wait(cross.at[b], x_recv.at[b])

    x_wait()
    for j in range(CH):
        for h in range(2):
            out_copy(j, h).wait()
    for d in range(4):
        for half in range(2):
            for copy in second_copies(CH - 1, half, d):
                copy.wait_send()

    def x_drain(slot, unused):
        for copy in x_copies(slot, jnp.where(slot == 0, 4, r), False):
            copy.wait_send()
        return unused

    lax.fori_loop(first_slot, 2, x_drain, 0)


def per_device(stiffness, coupling, slave_diag, slave_masters):
    any_space = pl.BlockSpec(memory_space=pl.ANY)
    vmem = pl.BlockSpec(memory_space=pltpu.VMEM)
    dma = pltpu.SemaphoreType.DMA
    flops = 2 * NB * (2 * NS * NS * FW + 3 * FW * FW * NS) // 4
    return pl.pallas_call(
        kernel,
        out_shape=(
            jax.ShapeDtypeStruct((NB, QF, FW), BF16),
            jax.ShapeDtypeStruct((1, QF, FW), BF16),
        ),
        in_specs=[any_space, any_space, vmem, vmem],
        out_specs=(any_space, any_space),
        scratch_shapes=[
            pltpu.VMEM((2, NS, NS), BF16),
            pltpu.VMEM((2, 2 * FW, NS), BF16),
            pltpu.VMEM((NB, QN, 2, FW), BF16),
            pltpu.VMEM((NB, 2 * FW, QN), BF16),
            pltpu.VMEM((2 * FW, QN), BF16),
            pltpu.VMEM((2, FW, NS), BF16),
            pltpu.VMEM((2, 3, FW, FW), BF16),
            pltpu.VMEM((CH, 2, 4, 4, 2, CR, HC), BF16),
            pltpu.VMEM((CH, 2, 3, 4, 2, CR, HC), BF16),
            pltpu.VMEM((CH, 2, 4, 2, CR, HC), BF16),
            pltpu.VMEM((CH, 2, 4, 2, CR, HC), BF16),
            pltpu.VMEM((QF, FW), BF16),
            pltpu.VMEM((2, 8, 128), jnp.int32),
            pltpu.VMEM((2, 2, 8, 128), jnp.int32),
            pltpu.SMEM((2, 2, 8, 128), jnp.int32),
            dma((NB,)), dma((2, ROWS)), dma((NB,)), dma((NB, 2)), dma((2, ROWS, 2)), dma((2,)), dma((2,)),
            dma((2, 2, CH, 8)), dma((CH, NONE)), dma((2, ROWS)), dma((NB,)),
            dma((CH, 2, 3)), dma((CH, 2, 3)), dma((CH, 2, 4, 2)), dma((CH, 2, 4, 2)),
            dma((CH, 2)), dma((2,)), dma, dma, pltpu.SemaphoreType.REGULAR,
            *[pltpu.VMEM((NONE + 1, CR, FW), BF16)] * CH,
        ],
        compiler_params=pltpu.CompilerParams(
            collective_id=0, has_side_effects=True, vmem_limit_bytes=58 * 2**20
        ),
        cost_estimate=pl.CostEstimate(flops=flops, bytes_accessed=9 * 2**20, transcendentals=0),
        name="condense",
    )(stiffness, coupling, slave_diag, slave_masters.T)


def solution(mesh):
    return jax.shard_map(
        per_device,
        mesh=mesh,
        in_specs=(
            P("col", "row", None),
            P("col", "row", None, None),
            P("col", "row"),
            P("col", None),
        ),
        out_specs=(P("col", "row", None), P("col", "row", None)),
        check_vma=False,
    )
```

```python
import functools

import jax
import jax.numpy as jnp
from jax import lax
from jax.experimental import pallas as pl
from jax.experimental.pallas import tpu as pltpu
from jax.sharding import PartitionSpec as P

MESH = pl.DeviceIdType.MESH
F32 = jnp.float32
BF16 = jnp.bfloat16
ROWS = 4
NB = 5
QN = 256
NS = 1024
FW = 768
QF = FW // ROWS
HF = QF // 2
HC = FW // 2
NONE = 4 * NB
CH = 6
CR = HF // CH


def kernel(
    stiff, coup, scale, masters,
    cross, diag,
    kbuf, pbuf, cin, ploc, relay, left, fills, dense, got1, part, got2, last, own_table, idx_v, idx_s,
    k_send, k_recv, c_sem, p_send, p_recv, r_send, r_recv, t_send, t_recv, x_send, x_recv,
    s1_send, s1_recv, s2_send, s2_recv, f_sem, i_sem, i_send, i_recv, ready, *terms,
):
    r = lax.axis_index("row")
    c = lax.axis_index("col")
    core = lax.rem(c, 2)
    y = lax.rem(c // 2, 4)
    z = c // 8
    other = c + 1 - 2 * core
    target = 2 * core
    through = target + 1
    far = lax.rem(target + 2, ROWS)

    def at_y(v, h=core):
        return z * 8 + v * 2 + h

    def at_z(v, h=core):
        return v * 8 + y * 2 + h

    def wait(ref, sem):
        pltpu.make_async_copy(ref, ref, sem).wait()

    def remote(src, dst, send, recv, device):
        return pltpu.make_async_remote_copy(
            src_ref=src, dst_ref=dst, send_sem=send, recv_sem=recv, device_id=device, device_id_type=MESH
        )

    order = [4] + [lax.rem(r + d, ROWS) for d in (1, 2, 3, 0)]
    loads = [pltpu.make_async_copy(coup.at[b], cin.at[b], c_sem.at[i]) for i, b in enumerate(order)]
    for load in loads:
        load.start()

    barrier = pltpu.get_barrier_semaphore()
    partners = [(r, other)]
    for d in (1, 2, 3):
        row = lax.rem(r + d, ROWS)
        partners += [(row, c), (row, other)]
        for h in (core, 1 - core):
            partners += [(r, at_y(lax.rem(y + d, 4), h)), (r, at_z(lax.rem(z + d, 4), h))]
    for device in partners:
        pl.semaphore_signal(barrier, inc=1, device_id=device, device_id_type=MESH)
    lane = lax.broadcasted_iota(jnp.int32, (8, 128), 1)
    low, high = jnp.full((8, 128), NONE, jnp.int32), jnp.full((8, 128), -1, jnp.int32)
    for e in range(2 * NB):
        hit = lane == jnp.broadcast_to(masters[pl.ds(e % 2, 1), pl.ds(e // 2, 1)], (8, 128))
        low = jnp.minimum(low, jnp.where(hit, core * 2 * NB + e, NONE))
        high = jnp.maximum(high, jnp.where(hit, core * 2 * NB + e, -1))
    own_table[0] = low
    own_table[1] = jnp.where(high > low, high, NONE)

    mine = pl.ds(pl.multiple_of(r * QN, QN), QN)

    def k_copy(b, slot, row):
        return remote(stiff.at[b], kbuf.at[slot, mine], k_send.at[slot], k_recv.at[slot], (row, c))

    def k_local(b, slot):
        return pltpu.make_async_copy(stiff.at[b], kbuf.at[slot, mine], k_recv.at[slot])

    def p_copy(b, slot, row, k):
        return remote(
            ploc.at[b, pl.ds(k * FW, FW)], pbuf.at[slot, pl.ds(k * FW, FW), mine],
            p_send.at[slot], p_recv.at[slot, k], (row, c),
        )

    def p_aside(k):
        return remote(
            ploc.at[4, pl.ds(k * FW, FW)], relay.at[pl.ds(k * FW, FW)],
            p_send.at[0], r_recv.at[k], (through, c),
        )

    def p_forward(k):
        return remote(
            relay.at[pl.ds(k * FW, FW)],
            pbuf.at[0, pl.ds(k * FW, FW), pl.ds(pl.multiple_of(far * QN, QN), QN)],
            r_send, p_recv.at[0, k], (target, c),
        )

    def p_local(b, slot, k):
        return pltpu.make_async_copy(
            ploc.at[b, pl.ds(k * FW, FW)], pbuf.at[slot, pl.ds(k * FW, FW), mine], p_recv.at[slot, k]
        )

    def send_block(i, remote_copy, local_copy, aside=None):
        if i == 0:
            @pl.when(r == target)
            def _():
                local_copy(4, 0).start()

            @pl.when((r != target) & (r != far if aside else True))
            def _():
                remote_copy(4, 0, target).start()

            if aside:
                @pl.when(r == far)
                def _():
                    aside().start()
        elif i == 3:
            @pl.when(r != through)
            def _():
                remote_copy(order[i], 1, order[i]).start()
        elif i < 4:
            remote_copy(order[i], 1, order[i]).start()
        else:
            local_copy(order[i], 1).start()

    def project(i, k):
        b = order[i]
        if k == 0:
            loads[i].wait()
        raw = cin[b, :, k, :].astype(F32).T
        ploc[b, pl.ds(k * FW, FW), :] = (raw / scale[pl.ds(b, 1), :]).astype(BF16)

    def p_start(i, k):
        send_block(
            i, functools.partial(p_copy, k=k), functools.partial(p_local, k=k), functools.partial(p_aside, k)
        )

    project(0, 0)
    project(0, 1)
    pl.semaphore_wait(barrier, len(partners))
    send_block(0, k_copy, k_local)
    p_start(0, 0)
    p_start(0, 1)
    for i in range(1, NB):
        send_block(i, k_copy, k_local)
    for k in range(2):
        for i in range(1, NB):
            project(i, k)
            p_start(i, k)

    own_idx = pltpu.make_async_copy(own_table, idx_v.at[core], i_sem.at[0])
    own_idx.start()
    idx_copy = remote(own_table, idx_v.at[core], i_send, i_recv, (r, other))
    idx_copy.start()

    for chunk in terms:
        chunk[NONE] = jnp.zeros((CR, FW), BF16)
    own_idx.wait()
    idx_copy.wait()
    to_smem = pltpu.make_async_copy(idx_v, idx_s, i_sem.at[1])
    to_smem.start()
    to_smem.wait()

    @pl.when(r == through)
    def _():
        for k in range(2):
            wait(relay.at[pl.ds(k * FW, FW)], r_recv.at[k])
            p_forward(k).start()
        k_copy(order[3], 1, order[3]).start()
        for k in range(2):
            p_copy(order[3], 1, order[3], k).start()

    def t_copies(slot, b, f, j):
        at = core * 2 * NB + b * 2 + f
        copies = []
        for dq in range(ROWS):
            for dh in range(2):
                q, h = lax.rem(r + dq, ROWS), lax.rem(core + dh, 2)
                src = fills.at[slot, f, pl.ds(pl.multiple_of(q * QF + h * HF + j * CR, CR), CR)]
                dst = terms[j].at[at]
                if dq or dh:
                    copies.append(remote(
                        src, dst, t_send.at[slot, j], t_recv.at[j], (q, c - core + h)
                    ))
                else:
                    copies.append(pltpu.make_async_copy(src, dst, t_recv.at[j]))
        return copies

    def x_copies(slot, b):
        copies = []
        for dq in range(ROWS):
            q = lax.rem(r + dq, ROWS)
            src = fills.at[slot, 2, pl.ds(pl.multiple_of(q * QF, QF), QF)]
            if dq:
                copies.append(remote(src, cross.at[b], x_send.at[slot], x_recv, (q, c)))
            else:
                copies.append(pltpu.make_async_copy(src, cross.at[b], x_recv))
        return copies

    def fill(slot, f, a, b):
        for n in range(3):
            out = lax.dot_general(
                left[a], pbuf[slot, pl.ds(b * FW + n * 256, 256), :],
                (((1,), (1,)), ((), ())), preferred_element_type=F32,
            )
            fills[slot, f, :, pl.ds(n * 256, 256)] = out.astype(BF16)

    def multiply(slot, k):
        for n in range(4):
            out = jnp.dot(
                pbuf[slot, pl.ds(k * FW, FW), :], kbuf[slot, :, pl.ds(n * 256, 256)],
                preferred_element_type=F32,
            )
            left[k, :, pl.ds(n * 256, 256)] = out.astype(BF16)

    def block(slot, unused):
        b = jnp.where(slot == 0, 4, r)

        def p_wait(k):
            wait(pbuf.at[slot, pl.ds(k * FW, FW)], p_recv.at[slot, k])

        def t_start(f, j):
            for copy in t_copies(slot, b, f, j):
                copy.start()

        def k_wait():
            wait(kbuf.at[slot], k_recv.at[slot])

        k_wait()
        p_wait(0)
        multiply(slot, 0)
        fill(slot, 0, 0, 0)
        p_wait(1)

        @pl.when(owner & (slot == 1))
        def _():
            for device in ring:
                pl.semaphore_signal(ready, inc=1, device_id=device, device_id_type=MESH)
            t_start(0, 0)

        multiply(slot, 1)
        fill(slot, 1, 1, 1)

        @pl.when(jnp.logical_not(owner))
        def _():
            fill(slot, 2, 0, 1)
            pl.semaphore_wait(ready, 2)

        @pl.when(jnp.logical_not(owner & (slot == 1)))
        def _():
            t_start(0, 0)

        t_start(1, 0)
        for j in range(1, CH):
            for f in range(2):
                t_start(f, j)

        @pl.when(owner)
        def _():
            fill(slot, 2, 0, 1)

        return unused

    owner = r == target
    def k_drain():
        wait(kbuf.at[1, pl.ds(0, 3 * QN)], k_send.at[1])
        wait(pbuf.at[1, pl.ds(0, 3 * FW // 2)], p_send.at[1])

        @pl.when(r != target)
        def _():
            wait(kbuf.at[1, pl.ds(0, QN)], k_send.at[0])
            wait(ploc.at[4], p_send.at[0])

        @pl.when(r == through)
        def _():
            wait(relay, r_send)

    def t_drain(j):
        def one(slot, unused):
            wait(terms[j].at[pl.ds(0, 14)], t_send.at[slot, j])
            return unused

        lax.fori_loop(first_slot, 2, one, 0)

    first_slot = jnp.where(owner, 0, 1)
    ring = [(r, other)] + [(lax.rem(r + d, ROWS), col) for d in (1, 2, 3) for col in (c, other)]
    lax.fori_loop(first_slot, 2, block, 0)
    for copy in x_copies(1, r):
        copy.start()

    @pl.when(r == target)
    def _():
        for copy in x_copies(0, 4):
            copy.start()
        pl.semaphore_wait(ready, 1)

    k_drain()


    place = (y, z)
    whom = (at_y, at_z)
    columns = (pl.ds(0, HC), pl.ds(HC, HC))

    def sum_terms(j, half, lead):
        chunk, cols = terms[j], columns[half]

        def one(n, unused):
            o, h = n // 2, lax.rem(n, 2)
            zz, yy = (o, lead) if half == 0 else (lead, o)
            m = zz * 8 + yy * 2 + h
            total = chunk[idx_s[0, 0, 0, m], :, cols].astype(F32) + chunk[idx_s[0, 1, 0, m], :, cols].astype(F32)
            total += chunk[idx_s[1, 0, 0, m], :, cols].astype(F32) + chunk[idx_s[1, 1, 0, m], :, cols].astype(F32)
            dense[j, half, lead, o, h] = total.astype(BF16)
            return unused

        lax.fori_loop(0, 8, one, 0)

    def first_copy(j, half, d):
        lead = lax.rem(place[half] + d, 4)
        return remote(
            dense.at[j, half, lead], got1.at[j, half, d - 1],
            s1_send.at[j], s1_recv.at[j], (r, whom[half](lead)),
        )

    def second_copies(j, half, d):
        o = lax.rem(place[1 - half] + d, 4)
        return [
            remote(
                part.at[j, half, o, h], got2.at[j, half, d, core],
                s2_send.at[j], s2_recv.at[j], (r, whom[1 - half](o, h)),
            )
            for h in (core, 1 - core)[0 if d else 1:]
        ]

    def t_wait(j):
        wait(terms[j].at[pl.ds(0, NONE)], t_recv.at[j])

    def first_wait(j):
        wait(got1.at[j], s1_recv.at[j])

    def second_wait(j):
        wait(got2.at[j], s2_recv.at[j])

    def stage0(j):
        t_wait(j)
        for d in (2, 1, 3, 0):
            for half in range(2):
                sum_terms(j, half, lax.rem(place[half] + d, 4))
                if d:
                    first_copy(j, half, d).start()

    def stage1(j):
        t_drain(j)
        first_wait(j)
        for half in range(2):
            for d in (2, 1, 3, 0):
                o = lax.rem(place[1 - half] + d, 4)
                total = dense[j, half, place[half], o].astype(F32)
                for e in range(3):
                    total += got1[j, half, e, o].astype(F32)
                part[j, half, o] = total.astype(BF16)
                for copy in second_copies(j, half, d):
                    copy.start()
            pltpu.make_async_copy(
                part.at[j, half, place[1 - half], core], got2.at[j, half, 0, core], s2_recv.at[j]
            ).start()

    def out_copy(j, h):
        rows = pl.ds(h * HF + j * CR, CR)
        return pltpu.make_async_copy(last.at[rows], diag.at[0, rows], f_sem)

    def second_drain(j):
        wait(terms[j].at[pl.ds(0, 7)], s2_send.at[j])

    def stage2(j):
        wait(got1.at[j], s1_send.at[j])
        if j:
            second_drain(j - 1)
        second_wait(j)
        for half in range(2):
            total = got2[j, half, 0].astype(F32)
            for d in (1, 2, 3):
                total += got2[j, half, d].astype(F32)
            total = total.astype(BF16)
            for h in range(2):
                last[pl.ds(h * HF + j * CR, CR), columns[half]] = total[h]
        for h in range(2):
            out_copy(j, h).start()

    stage0(0)
    stage0(1)
    stage1(0)
    for j in range(2, CH):
        stage0(j)
        stage1(j - 1)
        stage2(j - 2)
    stage1(CH - 1)
    stage2(CH - 2)
    stage2(CH - 1)

    def x_wait():
        wait(cross, x_recv)

    x_wait()
    second_drain(CH - 1)
    wait(cross.at[pl.ds(0, 3)], x_send.at[1])

    @pl.when(owner)
    def _():
        wait(cross.at[pl.ds(0, 3)], x_send.at[0])

    wait(diag, f_sem)


def per_device(stiffness, coupling, slave_diag, slave_masters):
    any_space = pl.BlockSpec(memory_space=pl.ANY)
    vmem = pl.BlockSpec(memory_space=pltpu.VMEM)
    dma = pltpu.SemaphoreType.DMA
    flops = 2 * NB * (2 * NS * NS * FW + 3 * FW * FW * NS) // 4
    return pl.pallas_call(
        kernel,
        out_shape=(
            jax.ShapeDtypeStruct((NB, QF, FW), BF16),
            jax.ShapeDtypeStruct((1, QF, FW), BF16),
        ),
        in_specs=[any_space, any_space, vmem, vmem],
        out_specs=(any_space, any_space),
        scratch_shapes=[
            pltpu.VMEM((2, NS, NS), BF16),
            pltpu.VMEM((2, 2 * FW, NS), BF16),
            pltpu.VMEM((NB, QN, 2, FW), BF16),
            pltpu.VMEM((NB, 2 * FW, QN), BF16),
            pltpu.VMEM((2 * FW, QN), BF16),
            pltpu.VMEM((2, FW, NS), BF16),
            pltpu.VMEM((2, 3, FW, FW), BF16),
            pltpu.VMEM((CH, 2, 4, 4, 2, CR, HC), BF16),
            pltpu.VMEM((CH, 2, 3, 4, 2, CR, HC), BF16),
            pltpu.VMEM((CH, 2, 4, 2, CR, HC), BF16),
            pltpu.VMEM((CH, 2, 4, 2, CR, HC), BF16),
            pltpu.VMEM((QF, FW), BF16),
            pltpu.VMEM((2, 8, 128), jnp.int32),
            pltpu.VMEM((2, 2, 8, 128), jnp.int32),
            pltpu.SMEM((2, 2, 8, 128), jnp.int32),
            dma((2,)), dma((2,)), dma((NB,)), dma((2,)), dma((2, 2)), dma, dma((2,)),
            dma((2, CH)), dma((CH,)), dma((2,)), dma,
            dma((CH,)), dma((CH,)), dma((CH,)), dma((CH,)), dma, dma((2,)), dma, dma, pltpu.SemaphoreType.REGULAR,
            *[pltpu.VMEM((NONE + 1, CR, FW), BF16)] * CH,
        ],
        compiler_params=pltpu.CompilerParams(
            collective_id=0, has_side_effects=True, vmem_limit_bytes=58 * 2**20
        ),
        cost_estimate=pl.CostEstimate(flops=flops, bytes_accessed=9 * 2**20, transcendentals=0),
        name="condense",
    )(stiffness, coupling, slave_diag, slave_masters.T)


def solution(mesh):
    return jax.shard_map(
        per_device,
        mesh=mesh,
        in_specs=(
            P("col", "row", None),
            P("col", "row", None, None),
            P("col", "row"),
            P("col", None),
        ),
        out_specs=(P("col", "row", None), P("col", "row", None)),
        check_vma=False,
    )
```

```python
import functools

import jax
import jax.numpy as jnp
from jax import lax
from jax.experimental import pallas as pl
from jax.experimental.pallas import tpu as pltpu
from jax.sharding import PartitionSpec as P

MESH = pl.DeviceIdType.MESH
F32 = jnp.float32
BF16 = jnp.bfloat16
ROWS = 4
NB = 5
QN = 256
NS = 1024
FW = 768
QF = FW // ROWS
HF = QF // 2
HC = FW // 2
NONE = 4 * NB
CH = 6
CR = HF // CH


def kernel(
    stiff, coup, scale, masters,
    cross, diag,
    kbuf, pbuf, cin, ploc, relay, x_relay, left, fills, dense, got1, part, got2, last, own_table, idx_v, idx_s,
    k_send, k_recv, c_sem, p_send, p_recv, r_send, r_recv, t_send, t_recv, x_send, x_recv, xr_send, xr_recv,
    s1_send, s1_recv, s2_send, s2_recv, f_sem, i_sem, i_send, i_recv, ready, *terms,
):
    r = lax.axis_index("row")
    c = lax.axis_index("col")
    core = lax.rem(c, 2)
    y = lax.rem(c // 2, 4)
    z = c // 8
    other = c + 1 - 2 * core
    target = 2 * core
    through = target + 1
    far = lax.rem(target + 2, ROWS)
    back = lax.rem(target + 3, ROWS)

    def at_y(v, h=core):
        return z * 8 + v * 2 + h

    def at_z(v, h=core):
        return v * 8 + y * 2 + h

    def wait(ref, sem):
        pltpu.make_async_copy(ref, ref, sem).wait()

    def remote(src, dst, send, recv, device):
        return pltpu.make_async_remote_copy(
            src_ref=src, dst_ref=dst, send_sem=send, recv_sem=recv, device_id=device, device_id_type=MESH
        )

    order = [4] + [lax.rem(r + d, ROWS) for d in (1, 2, 3, 0)]
    loads = [pltpu.make_async_copy(coup.at[b], cin.at[b], c_sem.at[i]) for i, b in enumerate(order)]
    for load in loads:
        load.start()

    barrier = pltpu.get_barrier_semaphore()
    partners = [(r, other)]
    for d in (1, 2, 3):
        row = lax.rem(r + d, ROWS)
        partners += [(row, c), (row, other)]
        for h in (core, 1 - core):
            partners += [(r, at_y(lax.rem(y + d, 4), h)), (r, at_z(lax.rem(z + d, 4), h))]
    for device in partners:
        pl.semaphore_signal(barrier, inc=1, device_id=device, device_id_type=MESH)
    lane = lax.broadcasted_iota(jnp.int32, (8, 128), 1)
    low, high = jnp.full((8, 128), NONE, jnp.int32), jnp.full((8, 128), -1, jnp.int32)
    for e in range(2 * NB):
        hit = lane == jnp.broadcast_to(masters[pl.ds(e % 2, 1), pl.ds(e // 2, 1)], (8, 128))
        low = jnp.minimum(low, jnp.where(hit, core * 2 * NB + e, NONE))
        high = jnp.maximum(high, jnp.where(hit, core * 2 * NB + e, -1))
    own_table[0] = low
    own_table[1] = jnp.where(high > low, high, NONE)

    mine = pl.ds(pl.multiple_of(r * QN, QN), QN)

    def k_copy(b, slot, row):
        return remote(stiff.at[b], kbuf.at[slot, mine], k_send.at[slot], k_recv.at[slot], (row, c))

    def k_local(b, slot):
        return pltpu.make_async_copy(stiff.at[b], kbuf.at[slot, mine], k_recv.at[slot])

    def p_copy(b, slot, row, k):
        return remote(
            ploc.at[b, pl.ds(k * FW, FW)], pbuf.at[slot, pl.ds(k * FW, FW), mine],
            p_send.at[slot], p_recv.at[slot, k], (row, c),
        )

    def p_aside(k):
        return remote(
            ploc.at[4, pl.ds(k * FW, FW)], relay.at[pl.ds(k * FW, FW)],
            p_send.at[0], r_recv.at[k], (through, c),
        )

    def p_forward(k):
        return remote(
            relay.at[pl.ds(k * FW, FW)],
            pbuf.at[0, pl.ds(k * FW, FW), pl.ds(pl.multiple_of(far * QN, QN), QN)],
            r_send, p_recv.at[0, k], (target, c),
        )

    def p_local(b, slot, k):
        return pltpu.make_async_copy(
            ploc.at[b, pl.ds(k * FW, FW)], pbuf.at[slot, pl.ds(k * FW, FW), mine], p_recv.at[slot, k]
        )

    def send_block(i, remote_copy, local_copy, aside=None):
        if i == 0:
            @pl.when(r == target)
            def _():
                local_copy(4, 0).start()

            @pl.when((r != target) & (r != far if aside else True))
            def _():
                remote_copy(4, 0, target).start()

            if aside:
                @pl.when(r == far)
                def _():
                    aside().start()
        elif i == 3:
            @pl.when(r != through)
            def _():
                remote_copy(order[i], 1, order[i]).start()
        elif i < 4:
            remote_copy(order[i], 1, order[i]).start()
        else:
            local_copy(order[i], 1).start()

    def project(i, k):
        b = order[i]
        if k == 0:
            loads[i].wait()
        raw = cin[b, :, k, :].astype(F32).T
        ploc[b, pl.ds(k * FW, FW), :] = (raw / scale[pl.ds(b, 1), :]).astype(BF16)

    def p_start(i, k):
        send_block(
            i, functools.partial(p_copy, k=k), functools.partial(p_local, k=k), functools.partial(p_aside, k)
        )

    project(0, 0)
    project(0, 1)
    pl.semaphore_wait(barrier, len(partners))
    send_block(0, k_copy, k_local)
    p_start(0, 0)
    p_start(0, 1)
    for i in range(1, NB):
        send_block(i, k_copy, k_local)
    for k in range(2):
        for i in range(1, NB):
            project(i, k)
            p_start(i, k)

    own_idx = pltpu.make_async_copy(own_table, idx_v.at[core], i_sem.at[0])
    own_idx.start()
    idx_copy = remote(own_table, idx_v.at[core], i_send, i_recv, (r, other))
    idx_copy.start()

    for chunk in terms:
        chunk[NONE] = jnp.zeros((CR, FW), BF16)
    own_idx.wait()
    idx_copy.wait()
    to_smem = pltpu.make_async_copy(idx_v, idx_s, i_sem.at[1])
    to_smem.start()
    to_smem.wait()

    @pl.when(r == through)
    def _():
        for k in range(2):
            wait(relay.at[pl.ds(k * FW, FW)], r_recv.at[k])
            p_forward(k).start()
        k_copy(order[3], 1, order[3]).start()
        for k in range(2):
            p_copy(order[3], 1, order[3], k).start()

    def t_copies(slot, b, f, j):
        at = core * 2 * NB + b * 2 + f
        copies = []
        for dq in range(ROWS):
            for dh in range(2):
                q, h = lax.rem(r + dq, ROWS), lax.rem(core + dh, 2)
                src = fills.at[slot, f, pl.ds(pl.multiple_of(q * QF + h * HF + j * CR, CR), CR)]
                dst = terms[j].at[at]
                if dq or dh:
                    copies.append(remote(
                        src, dst, t_send.at[slot, j], t_recv.at[j], (q, c - core + h)
                    ))
                else:
                    copies.append(pltpu.make_async_copy(src, dst, t_recv.at[j]))
        return copies

    def x_aside():
        src = fills.at[0, 2, pl.ds(pl.multiple_of(far * QF, QF), QF)]
        return remote(src, x_relay, x_send.at[0], xr_recv, (back, c))

    def x_forward():
        return remote(x_relay, cross.at[4], xr_send, x_recv, (far, c))

    def x_copies(slot, b):
        copies = []
        for dq in range(ROWS):
            if slot == 0 and dq == 2:
                continue
            q = lax.rem(r + dq, ROWS)
            src = fills.at[slot, 2, pl.ds(pl.multiple_of(q * QF, QF), QF)]
            if dq:
                copies.append(remote(src, cross.at[b], x_send.at[slot], x_recv, (q, c)))
            else:
                copies.append(pltpu.make_async_copy(src, cross.at[b], x_recv))
        return copies

    def fill(slot, f, a, b, skip=False):
        for n in range(3):
            out = lax.dot_general(
                left[a], pbuf[slot, pl.ds(b * FW + n * 256, 256), :],
                (((1,), (1,)), ((), ())), preferred_element_type=F32,
            ).astype(BF16)
            if skip:
                for q in range(2 * ROWS):
                    fills[slot, f, pl.ds(q * HF + CR, HF - CR), pl.ds(n * 256, 256)] = out[q * HF + CR:(q + 1) * HF]
            else:
                fills[slot, f, :, pl.ds(n * 256, 256)] = out

    def fill_head(f):
        rows = [pbuf[1, pl.ds(f * FW + q * HF, CR), :] for q in range(2 * ROWS)]
        head = jnp.dot(jnp.concatenate(rows), kbuf[1], preferred_element_type=F32).astype(BF16)
        out = lax.dot_general(
            head, pbuf[1, pl.ds(f * FW, FW), :], (((1,), (1,)), ((), ())), preferred_element_type=F32
        ).astype(BF16)
        for q in range(2 * ROWS):
            fills[1, f, pl.ds(q * HF, CR), :] = out[q * CR:(q + 1) * CR]

    def multiply(slot, k):
        for n in range(4):
            out = jnp.dot(
                pbuf[slot, pl.ds(k * FW, FW), :], kbuf[slot, :, pl.ds(n * 256, 256)],
                preferred_element_type=F32,
            )
            left[k, :, pl.ds(n * 256, 256)] = out.astype(BF16)

    def block(slot, unused):
        b = jnp.where(slot == 0, 4, r)

        def p_wait(k):
            wait(pbuf.at[slot, pl.ds(k * FW, FW)], p_recv.at[slot, k])

        def t_start(f, j):
            for copy in t_copies(slot, b, f, j):
                copy.start()

        def k_wait():
            wait(kbuf.at[slot], k_recv.at[slot])

        def tell(stage):
            for device in ring:
                pl.semaphore_signal(ready.at[stage], inc=1, device_id=device, device_id_type=MESH)

        k_wait()
        p_wait(0)
        multiply(slot, 0)
        fill(slot, 0, 0, 0)

        @pl.when(owner & (slot == 1))
        def _():
            tell(0)
            t_start(0, 0)
            p_wait(1)
            tell(1)
            fill_head(1)
            t_start(1, 0)
            multiply(slot, 1)
            fill(slot, 1, 1, 1, skip=True)

        @pl.when(jnp.logical_not(owner & (slot == 1)))
        def _():
            p_wait(1)
            multiply(slot, 1)
            fill(slot, 1, 1, 1)

            @pl.when(jnp.logical_not(owner))
            def _():
                fill(slot, 2, 0, 1)
                pl.semaphore_wait(ready.at[0], 2)

            t_start(0, 0)
            t_start(1, 0)

            @pl.when(jnp.logical_not(owner))
            def _():
                pl.semaphore_wait(ready.at[1], 2)

        for j in range(1, CH):
            for f in range(2):
                t_start(f, j)

        @pl.when(owner)
        def _():
            fill(slot, 2, 0, 1)

        @pl.when(slot == 0)
        def _():
            x_aside().start()

        return unused

    owner = r == target
    def k_drain():
        wait(kbuf.at[1, pl.ds(0, 3 * QN)], k_send.at[1])
        wait(pbuf.at[1, pl.ds(0, 3 * FW // 2)], p_send.at[1])

        @pl.when(r != target)
        def _():
            wait(kbuf.at[1, pl.ds(0, QN)], k_send.at[0])
            wait(ploc.at[4], p_send.at[0])

        @pl.when(r == through)
        def _():
            wait(relay, r_send)

    def t_drain(j):
        def one(slot, unused):
            wait(terms[j].at[pl.ds(0, 14)], t_send.at[slot, j])
            return unused

        lax.fori_loop(first_slot, 2, one, 0)

    first_slot = jnp.where(owner, 0, 1)
    ring = [(r, other)] + [(lax.rem(r + d, ROWS), col) for d in (1, 2, 3) for col in (c, other)]
    lax.fori_loop(first_slot, 2, block, 0)
    for copy in x_copies(1, r):
        copy.start()

    @pl.when(r == target)
    def _():
        for copy in x_copies(0, 4):
            copy.start()
        for stage in range(2):
            pl.semaphore_wait(ready.at[stage], 1)

    @pl.when(r == back)
    def _():
        wait(x_relay, xr_recv)
        x_forward().start()

    k_drain()


    place = (y, z)
    whom = (at_y, at_z)
    columns = (pl.ds(0, HC), pl.ds(HC, HC))

    def sum_terms(j, half, lead):
        chunk, cols = terms[j], columns[half]

        def one(n, unused):
            o, h = n // 2, lax.rem(n, 2)
            zz, yy = (o, lead) if half == 0 else (lead, o)
            m = zz * 8 + yy * 2 + h
            total = chunk[idx_s[0, 0, 0, m], :, cols].astype(F32) + chunk[idx_s[0, 1, 0, m], :, cols].astype(F32)
            total += chunk[idx_s[1, 0, 0, m], :, cols].astype(F32) + chunk[idx_s[1, 1, 0, m], :, cols].astype(F32)
            dense[j, half, lead, o, h] = total.astype(BF16)
            return unused

        lax.fori_loop(0, 8, one, 0)

    def first_copy(j, half, d):
        lead = lax.rem(place[half] + d, 4)
        return remote(
            dense.at[j, half, lead], got1.at[j, half, d - 1],
            s1_send.at[j], s1_recv.at[j], (r, whom[half](lead)),
        )

    def second_copies(j, half, d):
        o = lax.rem(place[1 - half] + d, 4)
        return [
            remote(
                part.at[j, half, o, h], got2.at[j, half, d, core],
                s2_send.at[j], s2_recv.at[j], (r, whom[1 - half](o, h)),
            )
            for h in (core, 1 - core)[0 if d else 1:]
        ]

    def t_wait(j):
        wait(terms[j].at[pl.ds(0, NONE)], t_recv.at[j])

    def first_wait(j):
        wait(got1.at[j], s1_recv.at[j])

    def second_wait(j):
        wait(got2.at[j], s2_recv.at[j])

    def stage0(j):
        t_wait(j)
        for d in (2, 1, 3, 0):
            for half in range(2):
                sum_terms(j, half, lax.rem(place[half] + d, 4))
                if d:
                    first_copy(j, half, d).start()

    def stage1(j):
        t_drain(j)
        first_wait(j)
        for half in range(2):
            for d in (2, 1, 3, 0):
                o = lax.rem(place[1 - half] + d, 4)
                total = dense[j, half, place[half], o].astype(F32)
                for e in range(3):
                    total += got1[j, half, e, o].astype(F32)
                part[j, half, o] = total.astype(BF16)
                for copy in second_copies(j, half, d):
                    copy.start()
            pltpu.make_async_copy(
                part.at[j, half, place[1 - half], core], got2.at[j, half, 0, core], s2_recv.at[j]
            ).start()

    def out_copy(j, h):
        rows = pl.ds(h * HF + j * CR, CR)
        return pltpu.make_async_copy(last.at[rows], diag.at[0, rows], f_sem)

    def second_drain(j):
        wait(terms[j].at[pl.ds(0, 7)], s2_send.at[j])

    def stage2(j):
        wait(got1.at[j], s1_send.at[j])
        if j:
            second_drain(j - 1)
        second_wait(j)
        for half in range(2):
            total = got2[j, half, 0].astype(F32)
            for d in (1, 2, 3):
                total += got2[j, half, d].astype(F32)
            total = total.astype(BF16)
            for h in range(2):
                last[pl.ds(h * HF + j * CR, CR), columns[half]] = total[h]
        for h in range(2):
            out_copy(j, h).start()

    stage0(0)
    stage0(1)
    stage1(0)
    for j in range(2, CH):
        stage0(j)
        stage1(j - 1)
        stage2(j - 2)
    stage1(CH - 1)
    stage2(CH - 2)
    stage2(CH - 1)

    def x_wait():
        wait(cross, x_recv)

    x_wait()
    second_drain(CH - 1)
    wait(cross.at[pl.ds(0, 3)], x_send.at[1])

    @pl.when(owner)
    def _():
        wait(cross.at[pl.ds(0, 3)], x_send.at[0])

    @pl.when(r == back)
    def _():
        wait(x_relay, xr_send)

    wait(diag, f_sem)


def per_device(stiffness, coupling, slave_diag, slave_masters):
    any_space = pl.BlockSpec(memory_space=pl.ANY)
    vmem = pl.BlockSpec(memory_space=pltpu.VMEM)
    dma = pltpu.SemaphoreType.DMA
    flops = 2 * NB * (2 * NS * NS * FW + 3 * FW * FW * NS) // 4
    return pl.pallas_call(
        kernel,
        out_shape=(pltpu.VMEM((NB, QF, FW), BF16), pltpu.VMEM((1, QF, FW), BF16)),
        in_specs=[any_space, any_space, vmem, vmem],
        out_specs=(vmem, vmem),
        scratch_shapes=[
            pltpu.VMEM((2, NS, NS), BF16),
            pltpu.VMEM((2, 2 * FW, NS), BF16),
            pltpu.VMEM((NB, QN, 2, FW), BF16),
            pltpu.VMEM((NB, 2 * FW, QN), BF16),
            pltpu.VMEM((2 * FW, QN), BF16),
            pltpu.VMEM((QF, FW), BF16),
            pltpu.VMEM((2, FW, NS), BF16),
            pltpu.VMEM((2, 3, FW, FW), BF16),
            pltpu.VMEM((CH, 2, 4, 4, 2, CR, HC), BF16),
            pltpu.VMEM((CH, 2, 3, 4, 2, CR, HC), BF16),
            pltpu.VMEM((CH, 2, 4, 2, CR, HC), BF16),
            pltpu.VMEM((CH, 2, 4, 2, CR, HC), BF16),
            pltpu.VMEM((QF, FW), BF16),
            pltpu.VMEM((2, 8, 128), jnp.int32),
            pltpu.VMEM((2, 2, 8, 128), jnp.int32),
            pltpu.SMEM((2, 2, 8, 128), jnp.int32),
            dma((2,)), dma((2,)), dma((NB,)), dma((2,)), dma((2, 2)), dma, dma((2,)),
            dma((2, CH)), dma((CH,)), dma((2,)), dma, dma, dma,
            dma((CH,)), dma((CH,)), dma((CH,)), dma((CH,)), dma, dma((2,)), dma, dma, pltpu.SemaphoreType.REGULAR((2,)),
            *[pltpu.VMEM((NONE + 1, CR, FW), BF16)] * CH,
        ],
        compiler_params=pltpu.CompilerParams(
            collective_id=0, has_side_effects=True, vmem_limit_bytes=58 * 2**20
        ),
        cost_estimate=pl.CostEstimate(flops=flops, bytes_accessed=9 * 2**20, transcendentals=0),
        name="condense",
    )(stiffness, coupling, slave_diag, slave_masters.T)


def solution(mesh):
    return jax.shard_map(
        per_device,
        mesh=mesh,
        in_specs=(
            P("col", "row", None),
            P("col", "row", None, None),
            P("col", "row"),
            P("col", None),
        ),
        out_specs=(P("col", "row", None), P("col", "row", None)),
        check_vma=False,
    )
```

```python
import functools

import jax
import jax.numpy as jnp
from jax import lax
from jax.experimental import pallas as pl
from jax.experimental.pallas import tpu as pltpu
from jax.sharding import PartitionSpec as P

MESH = pl.DeviceIdType.MESH
F32 = jnp.float32
BF16 = jnp.bfloat16
ROWS = 4
NB = 5
QN = 256
NS = 1024
FW = 768
QF = FW // ROWS
HF = QF // 2
HC = FW // 2
NONE = 4 * NB
CH = 6
CR = HF // CH
X_AT = 4


def kernel(
    stiff, coup, scale_in, masters_in,
    cross, diag,
    kbuf, pbuf, cin, scale, masters, ploc, relay, x_relay, left, fills, dense, hop, got1, part, got2,
    own_table, idx_v, idx_s,
    k_send, k_recv, c_sem, p_send, p_recv, r_send, r_recv, t_send, t_recv, x_send, x_recv, xr_send, xr_recv,
    s1_send, s1_recv, s2_send, s2_recv, h_recv, b_send, i_sem, i_send, i_recv, small, ready, *terms,
):
    r = lax.axis_index("row")
    c = lax.axis_index("col")
    core = lax.rem(c, 2)
    y = lax.rem(c // 2, 4)
    z = c // 8
    other = c + 1 - 2 * core
    target = 2 * core
    through = target + 1
    far = lax.rem(target + 2, ROWS)
    back = lax.rem(target + 3, ROWS)

    def at_y(v, h=core):
        return z * 8 + v * 2 + h

    def at_z(v, h=core):
        return v * 8 + y * 2 + h

    def wait(ref, sem):
        pltpu.make_async_copy(ref, ref, sem).wait()

    def remote(src, dst, send, recv, device):
        return pltpu.make_async_remote_copy(
            src_ref=src, dst_ref=dst, send_sem=send, recv_sem=recv, device_id=device, device_id_type=MESH
        )

    barrier = pltpu.get_barrier_semaphore()
    partners = [(r, other)]
    for d in (1, 2, 3):
        row = lax.rem(r + d, ROWS)
        partners += [(row, c), (row, other)]
        for h in (core, 1 - core):
            partners += [(r, at_y(lax.rem(y + d, 4), h)), (r, at_z(lax.rem(z + d, 4), h))]
    for device in partners:
        pl.semaphore_signal(barrier, inc=1, device_id=device, device_id_type=MESH)
    order = [4] + [lax.rem(r + d, ROWS) for d in (1, 2, 3, 0)]
    loads = [pltpu.make_async_copy(coup.at[b], cin.at[b], c_sem.at[i]) for i, b in enumerate(order)]
    for load in loads:
        load.start()
    small_loads = [
        pltpu.make_async_copy(scale_in, scale, small.at[0]), pltpu.make_async_copy(masters_in, masters, small.at[1])
    ]
    for load in small_loads:
        load.start()

    for load in small_loads:
        load.wait()
    lane = lax.broadcasted_iota(jnp.int32, (8, 128), 1)
    least, most = jnp.full((8, 128), NONE, jnp.int32), jnp.full((8, 128), -1, jnp.int32)
    for e in range(2 * NB):
        hit = lane == jnp.broadcast_to(masters[pl.ds(e % 2, 1), pl.ds(e // 2, 1)], (8, 128))
        least = jnp.minimum(least, jnp.where(hit, core * 2 * NB + e, NONE))
        most = jnp.maximum(most, jnp.where(hit, core * 2 * NB + e, -1))
    own_table[0] = least
    own_table[1] = jnp.where(most > least, most, NONE)

    mine = pl.ds(pl.multiple_of(r * QN, QN), QN)

    def k_copy(b, slot, row):
        return remote(stiff.at[b], kbuf.at[slot, mine], k_send.at[slot], k_recv.at[slot], (row, c))

    def k_local(b, slot):
        return pltpu.make_async_copy(stiff.at[b], kbuf.at[slot, mine], k_recv.at[slot])

    def p_copy(b, slot, row, k):
        return remote(
            ploc.at[b, pl.ds(k * FW, FW)], pbuf.at[slot, pl.ds(k * FW, FW), mine],
            p_send.at[slot], p_recv.at[slot, k], (row, c),
        )

    def p_aside(k):
        return remote(
            ploc.at[4, pl.ds(k * FW, FW)], relay.at[pl.ds(k * FW, FW)],
            p_send.at[0], r_recv.at[k], (through, c),
        )

    def p_forward(k):
        return remote(
            relay.at[pl.ds(k * FW, FW)],
            pbuf.at[0, pl.ds(k * FW, FW), pl.ds(pl.multiple_of(far * QN, QN), QN)],
            r_send, p_recv.at[0, k], (target, c),
        )

    def p_local(b, slot, k):
        return pltpu.make_async_copy(
            ploc.at[b, pl.ds(k * FW, FW)], pbuf.at[slot, pl.ds(k * FW, FW), mine], p_recv.at[slot, k]
        )

    def send_block(i, remote_copy, local_copy, aside=None):
        if i == 0:
            @pl.when(r == target)
            def _():
                local_copy(4, 0).start()

            @pl.when((r != target) & (r != far if aside else True))
            def _():
                remote_copy(4, 0, target).start()

            if aside:
                @pl.when(r == far)
                def _():
                    aside().start()
        elif i == 3:
            @pl.when(r != through)
            def _():
                remote_copy(order[i], 1, order[i]).start()
        elif i < 4:
            remote_copy(order[i], 1, order[i]).start()
        else:
            local_copy(order[i], 1).start()

    def project(i, k):
        b = order[i]
        if k == 0:
            loads[i].wait()
        raw = cin[b, :, k, :].astype(F32).T
        ploc[b, pl.ds(k * FW, FW), :] = (raw / scale[pl.ds(b, 1), :]).astype(BF16)

    def p_start(i, k):
        send_block(
            i, functools.partial(p_copy, k=k), functools.partial(p_local, k=k), functools.partial(p_aside, k)
        )

    project(0, 0)
    project(0, 1)
    pl.semaphore_wait(barrier, len(partners))
    send_block(0, k_copy, k_local)
    p_start(0, 0)
    p_start(0, 1)
    for i in range(1, NB):
        send_block(i, k_copy, k_local)
    for k in range(2):
        for i in range(1, NB):
            project(i, k)
            p_start(i, k)

    own_idx = pltpu.make_async_copy(own_table, idx_v.at[core], i_sem.at[0])
    own_idx.start()
    idx_copy = remote(own_table, idx_v.at[core], i_send, i_recv, (r, other))
    idx_copy.start()

    for chunk in terms:
        chunk[NONE] = jnp.zeros((CR, FW), BF16)
    own_idx.wait()
    idx_copy.wait()
    to_smem = pltpu.make_async_copy(idx_v, idx_s, i_sem.at[1])
    to_smem.start()
    to_smem.wait()

    @pl.when(r == through)
    def _():
        for k in range(2):
            wait(relay.at[pl.ds(k * FW, FW)], r_recv.at[k])
            p_forward(k).start()
        k_copy(order[3], 1, order[3]).start()
        for k in range(2):
            p_copy(order[3], 1, order[3], k).start()

    def t_copies(slot, b, f, j):
        at = core * 2 * NB + b * 2 + f
        copies = []
        for dq in range(ROWS):
            for dh in range(2):
                q, h = lax.rem(r + dq, ROWS), lax.rem(core + dh, 2)
                src = fills.at[slot, f, pl.ds(pl.multiple_of(q * QF + h * HF + j * CR, CR), CR)]
                dst = terms[j].at[at]
                if dq or dh:
                    copies.append(remote(
                        src, dst, t_send.at[slot, j], t_recv.at[j], (q, c - core + h)
                    ))
                else:
                    copies.append(pltpu.make_async_copy(src, dst, t_recv.at[j]))
        return copies

    def x_aside():
        src = fills.at[0, 2, pl.ds(pl.multiple_of(far * QF, QF), QF)]
        return remote(src, x_relay, x_send.at[0], xr_recv, (back, c))

    def x_forward():
        return remote(x_relay, cross.at[4], xr_send, x_recv, (far, c))

    def x_copies(slot, b):
        copies = []
        for dq in range(ROWS):
            if slot == 0 and dq == 2:
                continue
            q = lax.rem(r + dq, ROWS)
            src = fills.at[slot, 2, pl.ds(pl.multiple_of(q * QF, QF), QF)]
            if dq:
                copies.append(remote(src, cross.at[b], x_send.at[slot], x_recv, (q, c)))
            else:
                copies.append(pltpu.make_async_copy(src, cross.at[b], x_recv))
        return copies

    def fill(slot, f, a, b, skip=False):
        for n in range(3):
            out = lax.dot_general(
                left[a], pbuf[slot, pl.ds(b * FW + n * 256, 256), :],
                (((1,), (1,)), ((), ())), preferred_element_type=F32,
            ).astype(BF16)
            if skip:
                for q in range(2 * ROWS):
                    fills[slot, f, pl.ds(q * HF + CR, HF - CR), pl.ds(n * 256, 256)] = out[q * HF + CR:(q + 1) * HF]
            else:
                fills[slot, f, :, pl.ds(n * 256, 256)] = out

    def fill_head(f):
        rows = [pbuf[1, pl.ds(f * FW + q * HF, CR), :] for q in range(2 * ROWS)]
        head = jnp.dot(jnp.concatenate(rows), kbuf[1], preferred_element_type=F32).astype(BF16)
        out = lax.dot_general(
            head, pbuf[1, pl.ds(f * FW, FW), :], (((1,), (1,)), ((), ())), preferred_element_type=F32
        ).astype(BF16)
        for q in range(2 * ROWS):
            fills[1, f, pl.ds(q * HF, CR), :] = out[q * CR:(q + 1) * CR]

    def multiply(slot, k):
        for n in range(4):
            out = jnp.dot(
                pbuf[slot, pl.ds(k * FW, FW), :], kbuf[slot, :, pl.ds(n * 256, 256)],
                preferred_element_type=F32,
            )
            left[k, :, pl.ds(n * 256, 256)] = out.astype(BF16)

    def block(slot, unused):
        b = jnp.where(slot == 0, 4, r)

        def p_wait(k):
            wait(pbuf.at[slot, pl.ds(k * FW, FW)], p_recv.at[slot, k])

        def t_start(f, j):
            for copy in t_copies(slot, b, f, j):
                copy.start()

        def k_wait():
            wait(kbuf.at[slot], k_recv.at[slot])

        def tell(stage):
            for device in ring:
                pl.semaphore_signal(ready.at[stage], inc=1, device_id=device, device_id_type=MESH)

        k_wait()
        p_wait(0)
        multiply(slot, 0)
        fill(slot, 0, 0, 0)

        @pl.when(owner & (slot == 1))
        def _():
            tell(0)
            t_start(0, 0)
            p_wait(1)
            tell(1)
            fill_head(1)
            t_start(1, 0)
            multiply(slot, 1)
            fill(slot, 1, 1, 1, skip=True)

        @pl.when(jnp.logical_not(owner & (slot == 1)))
        def _():
            p_wait(1)
            multiply(slot, 1)
            fill(slot, 1, 1, 1)

            @pl.when(jnp.logical_not(owner))
            def _():
                fill(slot, 2, 0, 1)
                pl.semaphore_wait(ready.at[0], 2)

            t_start(0, 0)
            t_start(1, 0)

            @pl.when(jnp.logical_not(owner))
            def _():
                pl.semaphore_wait(ready.at[1], 2)

        for j in range(1, CH):
            for f in range(2):
                t_start(f, j)

        @pl.when(owner)
        def _():
            fill(slot, 2, 0, 1)

        @pl.when(slot == 0)
        def _():
            x_aside().start()

        return unused

    owner = r == target
    def k_drain():
        wait(kbuf.at[1, pl.ds(0, 3 * QN)], k_send.at[1])
        wait(pbuf.at[1, pl.ds(0, 3 * FW // 2)], p_send.at[1])

        @pl.when(r != target)
        def _():
            wait(kbuf.at[1, pl.ds(0, QN)], k_send.at[0])
            wait(ploc.at[4], p_send.at[0])

        @pl.when(r == through)
        def _():
            wait(relay, r_send)

    def t_drain(j):
        def one(slot, unused):
            wait(terms[j].at[pl.ds(0, 14)], t_send.at[slot, j])
            return unused

        lax.fori_loop(first_slot, 2, one, 0)

    first_slot = jnp.where(owner, 0, 1)
    ring = [(r, other)] + [(lax.rem(r + d, ROWS), col) for d in (1, 2, 3) for col in (c, other)]
    lax.fori_loop(first_slot, 2, block, 0)

    @pl.when(owner)
    def _():
        for stage in range(2):
            pl.semaphore_wait(ready.at[stage], 1)

    def x_start():
        for copy in x_copies(1, r):
            copy.start()

        @pl.when(owner)
        def _():
            for copy in x_copies(0, 4):
                copy.start()

        @pl.when(r == back)
        def _():
            wait(x_relay, xr_recv)
            x_forward().start()

    k_drain()


    place = (y, z)
    whom = (at_y, at_z)
    columns = (pl.ds(0, HC), pl.ds(HC, HC))

    def sum_terms(j, half, lead):
        chunk, cols = terms[j], columns[half]

        def one(n, unused):
            o, h = n // 2, lax.rem(n, 2)
            zz, yy = (o, lead) if half == 0 else (lead, o)
            m = zz * 8 + yy * 2 + h
            total = chunk[idx_s[0, 0, 0, m], :, cols].astype(F32) + chunk[idx_s[0, 1, 0, m], :, cols].astype(F32)
            total += chunk[idx_s[1, 0, 0, m], :, cols].astype(F32) + chunk[idx_s[1, 1, 0, m], :, cols].astype(F32)
            dense[j, half, lead, o, h] = total.astype(BF16)
            return unused

        lax.fori_loop(0, 8, one, 0)

    after, before, low, high = 1, 3, pl.ds(0, 2), pl.ds(2, 2)

    def lead_of(half, d):
        return lax.rem(place[half] + d, 4)

    def ring_copy(j, half, lead, part_of, dst, send, recv, d):
        return remote(
            dense.at[j, half, lead_of(half, lead), part_of], dst, send.at[j], recv.at[j],
            (r, whom[half](lead_of(half, d))),
        )

    def first_copies(j, half, d):
        if d == 2:
            return [
                ring_copy(j, half, 2, low, hop.at[j, half, 0], s1_send, h_recv, after),
                ring_copy(j, half, 2, high, hop.at[j, half, 1], s1_send, h_recv, before),
            ]
        if d == after:
            return [ring_copy(j, half, d, high, got1.at[j, half, 0, high], s1_send, s1_recv, d)]
        if d == before:
            return [ring_copy(j, half, d, low, got1.at[j, half, 1, low], s1_send, s1_recv, d)]
        return []

    def hop_wait(j):
        wait(hop.at[j], h_recv.at[j])

    def stage_hop(j):
        hop_wait(j)
        for half in range(2):
            for n, d, part_of in ((0, after, low), (1, before, high)):
                lead = lead_of(half, d)
                total = dense[j, half, lead, part_of].astype(F32) + hop[j, half, n].astype(F32)
                dense[j, half, lead, part_of] = total.astype(BF16)
                ring_copy(j, half, d, part_of, got1.at[j, half, n, part_of], b_send, s1_recv, d).start()

    def second_copies(j, half, d):
        o = lax.rem(place[1 - half] + d, 4)
        return [
            remote(
                part.at[j, half, o, h], got2.at[j, half, d, core],
                s2_send.at[j], s2_recv.at[j], (r, whom[1 - half](o, h)),
            )
            for h in (core, 1 - core)[0 if d else 1:]
        ]

    def t_wait(j):
        wait(terms[j].at[pl.ds(0, NONE)], t_recv.at[j])

    def first_wait(j):
        wait(got1.at[j], s1_recv.at[j])

    def second_wait(j):
        wait(got2.at[j], s2_recv.at[j])

    def stage0(j):
        t_wait(j)
        for d in (2, 1, 3, 0):
            for half in range(2):
                sum_terms(j, half, lax.rem(place[half] + d, 4))
                for copy in first_copies(j, half, d):
                    copy.start()

    def stage1(j):
        t_drain(j)
        first_wait(j)
        for half in range(2):
            for d in (2, 1, 3, 0):
                o = lax.rem(place[1 - half] + d, 4)
                total = dense[j, half, place[half], o].astype(F32)
                for e in range(2):
                    total += got1[j, half, e, o].astype(F32)
                part[j, half, o] = total.astype(BF16)
                for copy in second_copies(j, half, d):
                    copy.start()
            pltpu.make_async_copy(
                part.at[j, half, place[1 - half], core], got2.at[j, half, 0, core], s2_recv.at[j]
            ).start()

    def second_drain(j):
        wait(terms[j].at[pl.ds(0, 7)], s2_send.at[j])

    def stage2(j):
        wait(got1.at[j], s1_send.at[j])
        wait(hop.at[j], b_send.at[j])
        if j:
            second_drain(j - 1)
        second_wait(j)
        for half in range(2):
            total = got2[j, half, 0].astype(F32)
            for d in (1, 2, 3):
                total += got2[j, half, d].astype(F32)
            total = total.astype(BF16)
            for h in range(2):
                diag[0, pl.ds(h * HF + j * CR, CR), columns[half]] = total[h]

    for j in range(CH + 3):
        if j < CH:
            stage0(j)
        if j == X_AT:
            x_start()
        if 1 <= j <= CH:
            stage_hop(j - 1)
        if 2 <= j <= CH + 1:
            stage1(j - 2)
        if j >= 3:
            stage2(j - 3)

    def x_wait():
        wait(cross, x_recv)

    x_wait()
    second_drain(CH - 1)
    wait(cross.at[pl.ds(0, 3)], x_send.at[1])

    @pl.when(owner)
    def _():
        wait(cross.at[pl.ds(0, 3)], x_send.at[0])

    @pl.when(r == back)
    def _():
        wait(x_relay, xr_send)


def per_device(stiffness, coupling, slave_diag, slave_masters):
    any_space = pl.BlockSpec(memory_space=pl.ANY)
    vmem = pl.BlockSpec(memory_space=pltpu.VMEM)
    dma = pltpu.SemaphoreType.DMA
    flops = 2 * NB * (2 * NS * NS * FW + 3 * FW * FW * NS) // 4
    return pl.pallas_call(
        kernel,
        out_shape=(pltpu.VMEM((NB, QF, FW), BF16), pltpu.VMEM((1, QF, FW), BF16)),
        in_specs=[any_space] * 4,
        out_specs=(vmem, vmem),
        scratch_shapes=[
            pltpu.VMEM((2, NS, NS), BF16),
            pltpu.VMEM((2, 2 * FW, NS), BF16),
            pltpu.VMEM((NB, QN, 2, FW), BF16),
            pltpu.VMEM((NB, QN), F32),
            pltpu.VMEM((2, NB), jnp.int32),
            pltpu.VMEM((NB, 2 * FW, QN), BF16),
            pltpu.VMEM((2 * FW, QN), BF16),
            pltpu.VMEM((QF, FW), BF16),
            pltpu.VMEM((2, FW, NS), BF16),
            pltpu.VMEM((2, 3, FW, FW), BF16),
            pltpu.VMEM((CH, 2, 4, 4, 2, CR, HC), BF16),
            pltpu.VMEM((CH, 2, 2, 2, 2, CR, HC), BF16),
            pltpu.VMEM((CH, 2, 2, 4, 2, CR, HC), BF16),
            pltpu.VMEM((CH, 2, 4, 2, CR, HC), BF16),
            pltpu.VMEM((CH, 2, 4, 2, CR, HC), BF16),
            pltpu.VMEM((2, 8, 128), jnp.int32),
            pltpu.VMEM((2, 2, 8, 128), jnp.int32),
            pltpu.SMEM((2, 2, 8, 128), jnp.int32),
            dma((2,)), dma((2,)), dma((NB,)), dma((2,)), dma((2, 2)), dma, dma((2,)),
            dma((2, CH)), dma((CH,)), dma((2,)), dma, dma, dma,
            dma((CH,)), dma((CH,)), dma((CH,)), dma((CH,)), dma((CH,)), dma((CH,)), dma((2,)), dma, dma,
            dma((2,)), pltpu.SemaphoreType.REGULAR((2,)),
            *[pltpu.VMEM((NONE + 1, CR, FW), BF16)] * CH,
        ],
        compiler_params=pltpu.CompilerParams(
            collective_id=0, has_side_effects=True, vmem_limit_bytes=58 * 2**20
        ),
        cost_estimate=pl.CostEstimate(flops=flops, bytes_accessed=9 * 2**20, transcendentals=0),
        name="condense",
    )(stiffness, coupling, slave_diag, slave_masters.T)


def solution(mesh):
    return jax.shard_map(
        per_device,
        mesh=mesh,
        in_specs=(
            P("col", "row", None),
            P("col", "row", None, None),
            P("col", "row"),
            P("col", None),
        ),
        out_specs=(P("col", "row", None), P("col", "row", None)),
        check_vma=False,
    )
```

```python
import functools

import jax
import jax.numpy as jnp
from jax import lax
from jax.experimental import pallas as pl
from jax.experimental.pallas import tpu as pltpu
from jax.sharding import PartitionSpec as P

MESH = pl.DeviceIdType.MESH
F32 = jnp.float32
BF16 = jnp.bfloat16
ROWS = 4
NB = 5
QN = 256
NS = 1024
FW = 768
QF = FW // ROWS
HF = QF // 2
HC = FW // 2
NONE = 4 * NB
CH = 6
CR = HF // CH
X_AT = 4


def kernel(
    stiff, coup, scale_in, masters_in,
    cross, diag,
    kbuf, pbuf, cin, scale, masters, ploc, relay, x_relay, left, fills, dense, hop, got1, part, got2,
    own_table, idx_v, idx_s,
    k_send, k_recv, c_sem, p_send, p_recv, r_send, r_recv, t_send, t_recv, x_send, x_recv, xr_send, xr_recv,
    s1_send, s1_recv, s2_send, s2_recv, h_recv, b_send, i_sem, i_send, i_recv, small, ready, *terms,
):
    r = lax.axis_index("row")
    c = lax.axis_index("col")
    core = lax.rem(c, 2)
    y = lax.rem(c // 2, 4)
    z = c // 8
    other = c + 1 - 2 * core
    target = 2 * core
    through = target + 1
    far = lax.rem(target + 2, ROWS)
    back = lax.rem(target + 3, ROWS)

    def at_y(v, h=core):
        return z * 8 + v * 2 + h

    def at_z(v, h=core):
        return v * 8 + y * 2 + h

    def wait(ref, sem):
        pltpu.make_async_copy(ref, ref, sem).wait()

    def remote(src, dst, send, recv, device):
        return pltpu.make_async_remote_copy(
            src_ref=src, dst_ref=dst, send_sem=send, recv_sem=recv, device_id=device, device_id_type=MESH
        )

    barrier = pltpu.get_barrier_semaphore()
    partners = [(r, other)]
    for d in (1, 2, 3):
        row = lax.rem(r + d, ROWS)
        partners += [(row, c), (row, other)]
        for h in (core, 1 - core):
            partners += [(r, at_y(lax.rem(y + d, 4), h)), (r, at_z(lax.rem(z + d, 4), h))]
    for device in partners:
        pl.semaphore_signal(barrier, inc=1, device_id=device, device_id_type=MESH)
    order = [4] + [lax.rem(r + d, ROWS) for d in (1, 2, 3, 0)]
    loads = [pltpu.make_async_copy(coup.at[b], cin.at[b], c_sem.at[i]) for i, b in enumerate(order)]
    for load in loads:
        load.start()
    small_loads = [
        pltpu.make_async_copy(scale_in, scale, small.at[0]), pltpu.make_async_copy(masters_in, masters, small.at[1])
    ]
    for load in small_loads:
        load.start()

    for load in small_loads:
        load.wait()
    lane = lax.broadcasted_iota(jnp.int32, (8, 128), 1)
    least, most = jnp.full((8, 128), NONE, jnp.int32), jnp.full((8, 128), -1, jnp.int32)
    for e in range(2 * NB):
        hit = lane == jnp.broadcast_to(masters[pl.ds(e % 2, 1), pl.ds(e // 2, 1)], (8, 128))
        least = jnp.minimum(least, jnp.where(hit, core * 2 * NB + e, NONE))
        most = jnp.maximum(most, jnp.where(hit, core * 2 * NB + e, -1))
    own_table[0] = least
    own_table[1] = jnp.where(most > least, most, NONE)

    mine = pl.ds(pl.multiple_of(r * QN, QN), QN)

    def k_copy(b, slot, row):
        return remote(stiff.at[b], kbuf.at[slot, mine], k_send.at[slot], k_recv.at[slot], (row, c))

    def k_local(b, slot):
        return pltpu.make_async_copy(stiff.at[b], kbuf.at[slot, mine], k_recv.at[slot])

    def p_copy(b, slot, row, k):
        return remote(
            ploc.at[b, pl.ds(k * FW, FW)], pbuf.at[slot, pl.ds(k * FW, FW), mine],
            p_send.at[slot], p_recv.at[slot, k], (row, c),
        )

    def p_aside(k):
        return remote(
            ploc.at[4, pl.ds(k * FW, FW)], relay.at[pl.ds(k * FW, FW)],
            p_send.at[0], r_recv.at[k], (through, c),
        )

    def p_forward(k):
        return remote(
            relay.at[pl.ds(k * FW, FW)],
            pbuf.at[0, pl.ds(k * FW, FW), pl.ds(pl.multiple_of(far * QN, QN), QN)],
            r_send, p_recv.at[0, k], (target, c),
        )

    def p_local(b, slot, k):
        return pltpu.make_async_copy(
            ploc.at[b, pl.ds(k * FW, FW)], pbuf.at[slot, pl.ds(k * FW, FW), mine], p_recv.at[slot, k]
        )

    def send_block(i, remote_copy, local_copy, aside=None):
        if i == 0:
            @pl.when(r == target)
            def _():
                local_copy(4, 0).start()

            @pl.when((r != target) & (r != far if aside else True))
            def _():
                remote_copy(4, 0, target).start()

            if aside:
                @pl.when(r == far)
                def _():
                    aside().start()
        elif i == 3:
            @pl.when(r != through)
            def _():
                remote_copy(order[i], 1, order[i]).start()
        elif i < 4:
            remote_copy(order[i], 1, order[i]).start()
        else:
            local_copy(order[i], 1).start()

    def project(i, k):
        b = order[i]
        if k == 0:
            loads[i].wait()
        raw = cin[b, :, k, :].astype(F32).T
        ploc[b, pl.ds(k * FW, FW), :] = (raw / scale[pl.ds(b, 1), :]).astype(BF16)

    def p_start(i, k):
        send_block(
            i, functools.partial(p_copy, k=k), functools.partial(p_local, k=k), functools.partial(p_aside, k)
        )

    project(0, 0)
    project(0, 1)
    pl.semaphore_wait(barrier, len(partners))
    send_block(0, k_copy, k_local)
    p_start(0, 0)
    p_start(0, 1)
    for i in range(1, NB):
        send_block(i, k_copy, k_local)
    for k in range(2):
        for i in range(1, NB):
            project(i, k)
            p_start(i, k)

    own_idx = pltpu.make_async_copy(own_table, idx_v.at[core], i_sem.at[0])
    own_idx.start()
    idx_copy = remote(own_table, idx_v.at[core], i_send, i_recv, (r, other))
    idx_copy.start()

    for chunk in terms:
        chunk[NONE] = jnp.zeros((CR, FW), BF16)
    own_idx.wait()
    idx_copy.wait()
    to_smem = pltpu.make_async_copy(idx_v, idx_s, i_sem.at[1])
    to_smem.start()
    to_smem.wait()

    @pl.when(r == through)
    def _():
        for k in range(2):
            wait(relay.at[pl.ds(k * FW, FW)], r_recv.at[k])
            p_forward(k).start()
        k_copy(order[3], 1, order[3]).start()
        for k in range(2):
            p_copy(order[3], 1, order[3], k).start()

    def t_copies(slot, b, f, j):
        at = core * 2 * NB + b * 2 + f
        copies = []
        for dq in range(ROWS):
            for dh in range(2):
                q, h = lax.rem(r + dq, ROWS), lax.rem(core + dh, 2)
                src = fills.at[slot, f, pl.ds(pl.multiple_of(q * QF + h * HF + j * CR, CR), CR)]
                dst = terms[j].at[at]
                if dq or dh:
                    copies.append(remote(
                        src, dst, t_send.at[slot, j], t_recv.at[j], (q, c - core + h)
                    ))
                else:
                    copies.append(pltpu.make_async_copy(src, dst, t_recv.at[j]))
        return copies

    def x_aside():
        src = fills.at[0, 2, pl.ds(pl.multiple_of(far * QF, QF), QF)]
        return remote(src, x_relay, x_send.at[0], xr_recv, (back, c))

    def x_forward():
        return remote(x_relay, cross.at[4], xr_send, x_recv, (far, c))

    def x_copies(slot, b):
        copies = []
        for dq in range(ROWS):
            if slot == 0 and dq == 2:
                continue
            q = lax.rem(r + dq, ROWS)
            src = fills.at[slot, 2, pl.ds(pl.multiple_of(q * QF, QF), QF)]
            if dq:
                copies.append(remote(src, cross.at[b], x_send.at[slot], x_recv, (q, c)))
            else:
                copies.append(pltpu.make_async_copy(src, cross.at[b], x_recv))
        return copies

    def fill(slot, f, a, b, skip=False):
        for n in range(3):
            out = lax.dot_general(
                left[a], pbuf[slot, pl.ds(b * FW + n * 256, 256), :],
                (((1,), (1,)), ((), ())), preferred_element_type=F32,
            ).astype(BF16)
            if skip:
                for q in range(2 * ROWS):
                    fills[slot, f, pl.ds(q * HF + CR, HF - CR), pl.ds(n * 256, 256)] = out[q * HF + CR:(q + 1) * HF]
            else:
                fills[slot, f, :, pl.ds(n * 256, 256)] = out

    def fill_head(f):
        rows = [pbuf[1, pl.ds(f * FW + q * HF, CR), :] for q in range(2 * ROWS)]
        head = jnp.dot(jnp.concatenate(rows), kbuf[1], preferred_element_type=F32).astype(BF16)
        out = lax.dot_general(
            head, pbuf[1, pl.ds(f * FW, FW), :], (((1,), (1,)), ((), ())), preferred_element_type=F32
        ).astype(BF16)
        for q in range(2 * ROWS):
            fills[1, f, pl.ds(q * HF, CR), :] = out[q * CR:(q + 1) * CR]

    def multiply(slot, k):
        for n in range(4):
            out = jnp.dot(
                pbuf[slot, pl.ds(k * FW, FW), :], kbuf[slot, :, pl.ds(n * 256, 256)],
                preferred_element_type=F32,
            )
            left[k, :, pl.ds(n * 256, 256)] = out.astype(BF16)

    def block(slot, unused):
        b = jnp.where(slot == 0, 4, r)

        def p_wait(k):
            wait(pbuf.at[slot, pl.ds(k * FW, FW)], p_recv.at[slot, k])

        def t_start(f, j):
            for copy in t_copies(slot, b, f, j):
                copy.start()

        def k_wait():
            wait(kbuf.at[slot], k_recv.at[slot])

        def tell(stage):
            for device in ring:
                pl.semaphore_signal(ready.at[stage], inc=1, device_id=device, device_id_type=MESH)

        k_wait()
        p_wait(0)
        multiply(slot, 0)
        fill(slot, 0, 0, 0)

        @pl.when(owner & (slot == 1))
        def _():
            tell(0)
            t_start(0, 0)
            p_wait(1)
            tell(1)
            fill_head(1)
            t_start(1, 0)
            multiply(slot, 1)
            fill(slot, 1, 1, 1, skip=True)

        @pl.when(jnp.logical_not(owner & (slot == 1)))
        def _():
            p_wait(1)
            multiply(slot, 1)
            fill(slot, 1, 1, 1)

            @pl.when(jnp.logical_not(owner))
            def _():
                fill(slot, 2, 0, 1)
                pl.semaphore_wait(ready.at[0], 2)

            t_start(0, 0)
            t_start(1, 0)

            @pl.when(jnp.logical_not(owner))
            def _():
                pl.semaphore_wait(ready.at[1], 2)

        for j in range(1, CH):
            for f in range(2):
                t_start(f, j)

        @pl.when(owner)
        def _():
            fill(slot, 2, 0, 1)

        @pl.when(slot == 0)
        def _():
            x_aside().start()

        return unused

    owner = r == target
    def k_drain():
        wait(kbuf.at[1, pl.ds(0, 3 * QN)], k_send.at[1])
        wait(pbuf.at[1, pl.ds(0, 3 * FW // 2)], p_send.at[1])

        @pl.when(r != target)
        def _():
            wait(kbuf.at[1, pl.ds(0, QN)], k_send.at[0])
            wait(ploc.at[4], p_send.at[0])

        @pl.when(r == through)
        def _():
            wait(relay, r_send)

    def t_drain(j):
        def one(slot, unused):
            wait(terms[j].at[pl.ds(0, 14)], t_send.at[slot, j])
            return unused

        lax.fori_loop(first_slot, 2, one, 0)

    first_slot = jnp.where(owner, 0, 1)
    ring = [(r, other)] + [(lax.rem(r + d, ROWS), col) for d in (1, 2, 3) for col in (c, other)]
    lax.fori_loop(first_slot, 2, block, 0)

    @pl.when(owner)
    def _():
        for stage in range(2):
            pl.semaphore_wait(ready.at[stage], 1)

    def x_start():
        for copy in x_copies(1, r):
            copy.start()

        @pl.when(owner)
        def _():
            for copy in x_copies(0, 4):
                copy.start()

        @pl.when(r == back)
        def _():
            wait(x_relay, xr_recv)
            x_forward().start()

    k_drain()


    place = (y, z)
    whom = (at_y, at_z)
    columns = (pl.ds(0, HC), pl.ds(HC, HC))

    def sum_terms(j, half, lead):
        chunk, cols = terms[j], columns[half]

        def one(n, unused):
            o, h = n // 2, lax.rem(n, 2)
            zz, yy = (o, lead) if half == 0 else (lead, o)
            m = zz * 8 + yy * 2 + h
            total = chunk[idx_s[0, 0, 0, m], :, cols].astype(F32) + chunk[idx_s[0, 1, 0, m], :, cols].astype(F32)
            total += chunk[idx_s[1, 0, 0, m], :, cols].astype(F32) + chunk[idx_s[1, 1, 0, m], :, cols].astype(F32)
            dense[j, half, lead, o, h] = total.astype(BF16)
            return unused

        lax.fori_loop(0, 8, one, 0)

    after, before, low, high = 1, 3, pl.ds(0, 2), pl.ds(2, 2)

    def lead_of(half, d):
        return lax.rem(place[half] + d, 4)

    def ring_copy(j, half, lead, part_of, dst, send, recv, d):
        return remote(
            dense.at[j, half, lead_of(half, lead), part_of], dst, send.at[j], recv.at[j],
            (r, whom[half](lead_of(half, d))),
        )

    def first_copies(j, half, d):
        if d == 2:
            return [
                ring_copy(j, half, 2, low, hop.at[j, half, 0], s1_send, h_recv, after),
                ring_copy(j, half, 2, high, hop.at[j, half, 1], s1_send, h_recv, before),
            ]
        if d == after:
            return [ring_copy(j, half, d, high, got1.at[j, half, 0, high], s1_send, s1_recv, d)]
        if d == before:
            return [ring_copy(j, half, d, low, got1.at[j, half, 1, low], s1_send, s1_recv, d)]
        return []

    def hop_wait(j):
        wait(hop.at[j], h_recv.at[j])

    def stage_hop(j):
        hop_wait(j)
        for half in range(2):
            for n, d, part_of in ((0, after, low), (1, before, high)):
                lead = lead_of(half, d)
                total = dense[j, half, lead, part_of].astype(F32) + hop[j, half, n].astype(F32)
                dense[j, half, lead, part_of] = total.astype(BF16)
                ring_copy(j, half, d, part_of, got1.at[j, half, n, part_of], b_send, s1_recv, d).start()

    def second_copies(j, half, d):
        o = lax.rem(place[1 - half] + d, 4)
        return [
            remote(
                part.at[j, half, o, h], got2.at[j, half, d, core],
                s2_send.at[j], s2_recv.at[j], (r, whom[1 - half](o, h)),
            )
            for h in (core, 1 - core)[0 if d else 1:]
        ]

    def t_wait(j):
        wait(terms[j].at[pl.ds(0, NONE)], t_recv.at[j])

    def first_wait(j):
        wait(got1.at[j], s1_recv.at[j])

    def second_wait(j):
        wait(got2.at[j], s2_recv.at[j])

    def stage0(j):
        t_wait(j)
        for d in (2, 1, 3, 0):
            for half in range(2):
                sum_terms(j, half, lax.rem(place[half] + d, 4))
                for copy in first_copies(j, half, d):
                    copy.start()

    def stage1(j):
        t_drain(j)
        first_wait(j)
        for half in range(2):
            for d in (2, 1, 3, 0):
                o = lax.rem(place[1 - half] + d, 4)
                total = dense[j, half, place[half], o].astype(F32)
                for e in range(2):
                    total += got1[j, half, e, o].astype(F32)
                part[j, half, o] = total.astype(BF16)
                for copy in second_copies(j, half, d):
                    copy.start()
            pltpu.make_async_copy(
                part.at[j, half, place[1 - half], core], got2.at[j, half, 0, core], s2_recv.at[j]
            ).start()

    def second_drain(j):
        wait(terms[j].at[pl.ds(0, 7)], s2_send.at[j])

    def stage2(j):
        wait(got1.at[j], s1_send.at[j])
        wait(hop.at[j], b_send.at[j])
        if j:
            second_drain(j - 1)
        second_wait(j)
        for half in range(2):
            total = got2[j, half, 0].astype(F32)
            for d in (1, 2, 3):
                total += got2[j, half, d].astype(F32)
            total = total.astype(BF16)
            for h in range(2):
                diag[0, pl.ds(h * HF + j * CR, CR), columns[half]] = total[h]

    for j in range(CH + 3):
        if j < CH:
            stage0(j)
        if j == X_AT:
            x_start()
        if 1 <= j <= CH:
            stage_hop(j - 1)
        if 2 <= j <= CH + 1:
            stage1(j - 2)
        if j >= 3:
            stage2(j - 3)

    def x_wait():
        wait(cross, x_recv)

    x_wait()
    second_drain(CH - 1)
    wait(cross.at[pl.ds(0, 3)], x_send.at[1])

    @pl.when(owner)
    def _():
        wait(cross.at[pl.ds(0, 3)], x_send.at[0])

    @pl.when(r == back)
    def _():
        wait(x_relay, xr_send)


def store(cross, diag, cross_out, diag_out, sem):
    copies = [pltpu.make_async_copy(cross.at[b], cross_out.at[b], sem.at[b]) for b in range(NB)]
    copies.append(pltpu.make_async_copy(diag, diag_out, sem.at[NB]))
    for copy in copies:
        copy.start()
    for copy in copies:
        copy.wait()


def per_device(stiffness, coupling, slave_diag, slave_masters):
    any_space = pl.BlockSpec(memory_space=pl.ANY)
    vmem = pl.BlockSpec(memory_space=pltpu.VMEM)
    dma = pltpu.SemaphoreType.DMA
    flops = 2 * NB * (2 * NS * NS * FW + 3 * FW * FW * NS) // 4
    cross, diag = pl.pallas_call(
        kernel,
        out_shape=(pltpu.VMEM((NB, QF, FW), BF16), pltpu.VMEM((1, QF, FW), BF16)),
        in_specs=[any_space] * 4,
        out_specs=(vmem, vmem),
        scratch_shapes=[
            pltpu.VMEM((2, NS, NS), BF16),
            pltpu.VMEM((2, 2 * FW, NS), BF16),
            pltpu.VMEM((NB, QN, 2, FW), BF16),
            pltpu.VMEM((NB, QN), F32),
            pltpu.VMEM((2, NB), jnp.int32),
            pltpu.VMEM((NB, 2 * FW, QN), BF16),
            pltpu.VMEM((2 * FW, QN), BF16),
            pltpu.VMEM((QF, FW), BF16),
            pltpu.VMEM((2, FW, NS), BF16),
            pltpu.VMEM((2, 3, FW, FW), BF16),
            pltpu.VMEM((CH, 2, 4, 4, 2, CR, HC), BF16),
            pltpu.VMEM((CH, 2, 2, 2, 2, CR, HC), BF16),
            pltpu.VMEM((CH, 2, 2, 4, 2, CR, HC), BF16),
            pltpu.VMEM((CH, 2, 4, 2, CR, HC), BF16),
            pltpu.VMEM((CH, 2, 4, 2, CR, HC), BF16),
            pltpu.VMEM((2, 8, 128), jnp.int32),
            pltpu.VMEM((2, 2, 8, 128), jnp.int32),
            pltpu.SMEM((2, 2, 8, 128), jnp.int32),
            dma((2,)), dma((2,)), dma((NB,)), dma((2,)), dma((2, 2)), dma, dma((2,)),
            dma((2, CH)), dma((CH,)), dma((2,)), dma, dma, dma,
            dma((CH,)), dma((CH,)), dma((CH,)), dma((CH,)), dma((CH,)), dma((CH,)), dma((2,)), dma, dma,
            dma((2,)), pltpu.SemaphoreType.REGULAR((2,)),
            *[pltpu.VMEM((NONE + 1, CR, FW), BF16)] * CH,
        ],
        compiler_params=pltpu.CompilerParams(
            collective_id=0, has_side_effects=True, vmem_limit_bytes=58 * 2**20
        ),
        cost_estimate=pl.CostEstimate(flops=flops, bytes_accessed=9 * 2**20, transcendentals=0),
        name="condense",
    )(stiffness, coupling, slave_diag, slave_masters.T)
    cross = pltpu.with_memory_space_constraint(cross, pltpu.VMEM)
    diag = pltpu.with_memory_space_constraint(diag, pltpu.VMEM)
    return pl.pallas_call(
        store,
        out_shape=(
            jax.ShapeDtypeStruct((NB, QF, FW), BF16),
            jax.ShapeDtypeStruct((1, QF, FW), BF16),
        ),
        in_specs=[vmem, vmem],
        out_specs=(any_space, any_space),
        scratch_shapes=[dma((NB + 1,))],
        cost_estimate=pl.CostEstimate(flops=0, bytes_accessed=4 * 2**20, transcendentals=0),
        name="store",
    )(cross, diag)


def solution(mesh):
    return jax.shard_map(
        per_device,
        mesh=mesh,
        in_specs=(
            P("col", "row", None),
            P("col", "row", None, None),
            P("col", "row"),
            P("col", None),
        ),
        out_specs=(P("col", "row", None), P("col", "row", None)),
        check_vma=False,
    )
```

```python
import functools

import jax
import jax.numpy as jnp
from jax import lax
from jax.experimental import pallas as pl
from jax.experimental.pallas import tpu as pltpu
from jax.sharding import PartitionSpec as P

MESH = pl.DeviceIdType.MESH
F32 = jnp.float32
BF16 = jnp.bfloat16
ROWS = 4
NB = 5
QN = 256
NS = 1024
FW = 768
QF = FW // ROWS
HF = QF // 2
HC = FW // 2
NONE = 4 * NB
CH = 6
CR = HF // CH
X_AT = 3


def kernel(
    stiff, coup, scale_in, masters_in,
    cross, diag,
    kbuf, pbuf, cin, scale, masters, ploc, relay, x_relay, left, fills, dense, hop, got1, part, got2,
    own_table, idx_v, idx_s,
    k_send, k_recv, c_sem, p_send, p_recv, r_send, r_recv, t_send, t_recv, x_send, x_recv, xr_send, xr_recv,
    s1_send, s1_recv, s2_send, s2_recv, h_recv, b_send, i_sem, i_send, i_recv, small, ready, *terms,
):
    r = lax.axis_index("row")
    c = lax.axis_index("col")
    core = lax.rem(c, 2)
    y = lax.rem(c // 2, 4)
    z = c // 8
    other = c + 1 - 2 * core
    target = 2 * core
    through = target + 1
    far = lax.rem(target + 2, ROWS)
    back = lax.rem(target + 3, ROWS)

    def at_y(v, h=core):
        return z * 8 + v * 2 + h

    def at_z(v, h=core):
        return v * 8 + y * 2 + h

    def wait(ref, sem):
        pltpu.make_async_copy(ref, ref, sem).wait()

    def remote(src, dst, send, recv, device):
        return pltpu.make_async_remote_copy(
            src_ref=src, dst_ref=dst, send_sem=send, recv_sem=recv, device_id=device, device_id_type=MESH
        )

    barrier = pltpu.get_barrier_semaphore()
    partners = [(r, other)]
    for d in (1, 2, 3):
        row = lax.rem(r + d, ROWS)
        partners += [(row, c), (row, other)]
        for h in (core, 1 - core):
            partners += [(r, at_y(lax.rem(y + d, 4), h)), (r, at_z(lax.rem(z + d, 4), h))]
    for device in partners:
        pl.semaphore_signal(barrier, inc=1, device_id=device, device_id_type=MESH)
    order = [4] + [lax.rem(r + d, ROWS) for d in (1, 2, 3, 0)]
    loads = [pltpu.make_async_copy(coup.at[b], cin.at[b], c_sem.at[i]) for i, b in enumerate(order)]
    for load in loads:
        load.start()
    small_loads = [
        pltpu.make_async_copy(scale_in, scale, small.at[0]), pltpu.make_async_copy(masters_in, masters, small.at[1])
    ]
    for load in small_loads:
        load.start()

    for load in small_loads:
        load.wait()
    lane = lax.broadcasted_iota(jnp.int32, (8, 128), 1)
    least, most = jnp.full((8, 128), NONE, jnp.int32), jnp.full((8, 128), -1, jnp.int32)
    for e in range(2 * NB):
        hit = lane == jnp.broadcast_to(masters[pl.ds(e % 2, 1), pl.ds(e // 2, 1)], (8, 128))
        least = jnp.minimum(least, jnp.where(hit, core * 2 * NB + e, NONE))
        most = jnp.maximum(most, jnp.where(hit, core * 2 * NB + e, -1))
    own_table[0] = least
    own_table[1] = jnp.where(most > least, most, NONE)

    mine = pl.ds(pl.multiple_of(r * QN, QN), QN)

    def k_copy(b, slot, row):
        return remote(stiff.at[b], kbuf.at[slot, mine], k_send.at[slot], k_recv.at[slot], (row, c))

    def k_local(b, slot):
        return pltpu.make_async_copy(stiff.at[b], kbuf.at[slot, mine], k_recv.at[slot])

    def p_copy(b, slot, row, k):
        return remote(
            ploc.at[b, pl.ds(k * FW, FW)], pbuf.at[slot, pl.ds(k * FW, FW), mine],
            p_send.at[slot], p_recv.at[slot, k], (row, c),
        )

    def p_aside(k):
        return remote(
            ploc.at[4, pl.ds(k * FW, FW)], relay.at[pl.ds(k * FW, FW)],
            p_send.at[0], r_recv.at[k], (through, c),
        )

    def p_forward(k):
        return remote(
            relay.at[pl.ds(k * FW, FW)],
            pbuf.at[0, pl.ds(k * FW, FW), pl.ds(pl.multiple_of(far * QN, QN), QN)],
            r_send, p_recv.at[0, k], (target, c),
        )

    def p_local(b, slot, k):
        return pltpu.make_async_copy(
            ploc.at[b, pl.ds(k * FW, FW)], pbuf.at[slot, pl.ds(k * FW, FW), mine], p_recv.at[slot, k]
        )

    def send_block(i, remote_copy, local_copy, aside=None):
        if i == 0:
            @pl.when(r == target)
            def _():
                local_copy(4, 0).start()

            @pl.when((r != target) & (r != far if aside else True))
            def _():
                remote_copy(4, 0, target).start()

            if aside:
                @pl.when(r == far)
                def _():
                    aside().start()
        elif i == 3:
            @pl.when(r != through)
            def _():
                remote_copy(order[i], 1, order[i]).start()
        elif i < 4:
            remote_copy(order[i], 1, order[i]).start()
        else:
            local_copy(order[i], 1).start()

    def project(i, k):
        b = order[i]
        if k == 0:
            loads[i].wait()
        raw = cin[b, :, k, :].astype(F32).T
        ploc[b, pl.ds(k * FW, FW), :] = (raw / scale[pl.ds(b, 1), :]).astype(BF16)

    def p_start(i, k):
        send_block(
            i, functools.partial(p_copy, k=k), functools.partial(p_local, k=k), functools.partial(p_aside, k)
        )

    project(0, 0)
    project(0, 1)
    pl.semaphore_wait(barrier, len(partners))
    send_block(0, k_copy, k_local)
    p_start(0, 0)
    p_start(0, 1)
    for i in range(1, NB):
        send_block(i, k_copy, k_local)
    for k in range(2):
        for i in range(1, NB):
            project(i, k)
            p_start(i, k)

    own_idx = pltpu.make_async_copy(own_table, idx_v.at[core], i_sem.at[0])
    own_idx.start()
    idx_copy = remote(own_table, idx_v.at[core], i_send, i_recv, (r, other))
    idx_copy.start()

    for chunk in terms:
        chunk[NONE] = jnp.zeros((CR, FW), BF16)
    own_idx.wait()
    idx_copy.wait()
    to_smem = pltpu.make_async_copy(idx_v, idx_s, i_sem.at[1])
    to_smem.start()
    to_smem.wait()

    @pl.when(r == through)
    def _():
        for k in range(2):
            wait(relay.at[pl.ds(k * FW, FW)], r_recv.at[k])
            p_forward(k).start()
        k_copy(order[3], 1, order[3]).start()
        for k in range(2):
            p_copy(order[3], 1, order[3], k).start()

    def t_copies(slot, b, f, j):
        at = core * 2 * NB + b * 2 + f
        copies = []
        for dq in range(ROWS):
            for dh in range(2):
                q, h = lax.rem(r + dq, ROWS), lax.rem(core + dh, 2)
                src = fills.at[slot, f, pl.ds(pl.multiple_of(q * QF + h * HF + j * CR, CR), CR)]
                dst = terms[j].at[at]
                if dq or dh:
                    copies.append(remote(
                        src, dst, t_send.at[slot, j], t_recv.at[j], (q, c - core + h)
                    ))
                else:
                    copies.append(pltpu.make_async_copy(src, dst, t_recv.at[j]))
        return copies

    def x_aside():
        src = fills.at[0, 2, pl.ds(pl.multiple_of(far * QF, QF), QF)]
        return remote(src, x_relay, x_send.at[0], xr_recv, (back, c))

    def x_forward():
        return remote(x_relay, cross.at[4], xr_send, x_recv, (far, c))

    def x_copies(slot, b, places):
        copies = []
        for dq in places:
            q = lax.rem(r + dq, ROWS)
            src = fills.at[slot, 2, pl.ds(pl.multiple_of(q * QF, QF), QF)]
            if dq:
                copies.append(remote(src, cross.at[b], x_send.at[slot], x_recv, (q, c)))
            else:
                copies.append(pltpu.make_async_copy(src, cross.at[b], x_recv))
        return copies

    def fill(slot, f, a, b, skip=False):
        for n in range(3):
            out = lax.dot_general(
                left[a], pbuf[slot, pl.ds(b * FW + n * 256, 256), :],
                (((1,), (1,)), ((), ())), preferred_element_type=F32,
            ).astype(BF16)
            if skip:
                for q in range(2 * ROWS):
                    fills[slot, f, pl.ds(q * HF + CR, HF - CR), pl.ds(n * 256, 256)] = out[q * HF + CR:(q + 1) * HF]
            else:
                fills[slot, f, :, pl.ds(n * 256, 256)] = out

    def fill_head(f):
        rows = [pbuf[1, pl.ds(f * FW + q * HF, CR), :] for q in range(2 * ROWS)]
        head = jnp.dot(jnp.concatenate(rows), kbuf[1], preferred_element_type=F32).astype(BF16)
        out = lax.dot_general(
            head, pbuf[1, pl.ds(f * FW, FW), :], (((1,), (1,)), ((), ())), preferred_element_type=F32
        ).astype(BF16)
        for q in range(2 * ROWS):
            fills[1, f, pl.ds(q * HF, CR), :] = out[q * CR:(q + 1) * CR]

    def multiply(slot, k):
        for n in range(4):
            out = jnp.dot(
                pbuf[slot, pl.ds(k * FW, FW), :], kbuf[slot, :, pl.ds(n * 256, 256)],
                preferred_element_type=F32,
            )
            left[k, :, pl.ds(n * 256, 256)] = out.astype(BF16)

    def block(slot, unused):
        b = jnp.where(slot == 0, 4, r)

        def p_wait(k):
            wait(pbuf.at[slot, pl.ds(k * FW, FW)], p_recv.at[slot, k])

        def t_start(f, j):
            for copy in t_copies(slot, b, f, j):
                copy.start()

        def k_wait():
            wait(kbuf.at[slot], k_recv.at[slot])

        def tell(stage):
            for device in ring:
                pl.semaphore_signal(ready.at[stage], inc=1, device_id=device, device_id_type=MESH)

        k_wait()
        p_wait(0)
        multiply(slot, 0)
        fill(slot, 0, 0, 0)

        @pl.when(owner & (slot == 1))
        def _():
            tell(0)
            t_start(0, 0)
            p_wait(1)
            tell(1)
            fill_head(1)
            t_start(1, 0)
            multiply(slot, 1)
            fill(slot, 1, 1, 1, skip=True)

        @pl.when(jnp.logical_not(owner & (slot == 1)))
        def _():
            p_wait(1)
            multiply(slot, 1)
            fill(slot, 1, 1, 1)

            @pl.when(jnp.logical_not(owner))
            def _():
                fill(slot, 2, 0, 1)
                pl.semaphore_wait(ready.at[0], 2)

            t_start(0, 0)
            t_start(1, 0)

            @pl.when(jnp.logical_not(owner))
            def _():
                pl.semaphore_wait(ready.at[1], 2)

        for j in range(1, CH):
            for f in range(2):
                t_start(f, j)

        @pl.when(owner)
        def _():
            fill(slot, 2, 0, 1)

        @pl.when(slot == 0)
        def _():
            x_aside().start()

        return unused

    owner = r == target
    def k_drain():
        wait(kbuf.at[1, pl.ds(0, 3 * QN)], k_send.at[1])
        wait(pbuf.at[1, pl.ds(0, 3 * FW // 2)], p_send.at[1])

        @pl.when(r != target)
        def _():
            wait(kbuf.at[1, pl.ds(0, QN)], k_send.at[0])
            wait(ploc.at[4], p_send.at[0])

        @pl.when(r == through)
        def _():
            wait(relay, r_send)

    def t_drain(j):
        def one(slot, unused):
            wait(terms[j].at[pl.ds(0, 14)], t_send.at[slot, j])
            return unused

        lax.fori_loop(first_slot, 2, one, 0)

    first_slot = jnp.where(owner, 0, 1)
    ring = [(r, other)] + [(lax.rem(r + d, ROWS), col) for d in (1, 2, 3) for col in (c, other)]
    lax.fori_loop(first_slot, 2, block, 0)

    @pl.when(owner)
    def _():
        for stage in range(2):
            pl.semaphore_wait(ready.at[stage], 1)

    for copy in x_copies(1, r, (2,)):
        copy.start()

    def x_start():
        for copy in x_copies(1, r, (0, 1, 3)):
            copy.start()

        @pl.when(owner)
        def _():
            for copy in x_copies(0, 4, (0, 1, 3)):
                copy.start()

        @pl.when(r == back)
        def _():
            wait(x_relay, xr_recv)
            x_forward().start()

    k_drain()


    place = (y, z)
    whom = (at_y, at_z)
    columns = (pl.ds(0, HC), pl.ds(HC, HC))

    def sum_terms(j, half, lead):
        chunk, cols = terms[j], columns[half]

        def one(n, unused):
            o, h = n // 2, lax.rem(n, 2)
            zz, yy = (o, lead) if half == 0 else (lead, o)
            m = zz * 8 + yy * 2 + h
            total = chunk[idx_s[0, 0, 0, m], :, cols].astype(F32) + chunk[idx_s[0, 1, 0, m], :, cols].astype(F32)
            total += chunk[idx_s[1, 0, 0, m], :, cols].astype(F32) + chunk[idx_s[1, 1, 0, m], :, cols].astype(F32)
            dense[j, half, lead, o, h] = total.astype(BF16)
            return unused

        lax.fori_loop(0, 8, one, 0)

    after, before, low, high = 1, 3, pl.ds(0, 2), pl.ds(2, 2)

    def lead_of(half, d):
        return lax.rem(place[half] + d, 4)

    def ring_copy(j, half, lead, part_of, dst, send, recv, d):
        return remote(
            dense.at[j, half, lead_of(half, lead), part_of], dst, send.at[j], recv.at[j],
            (r, whom[half](lead_of(half, d))),
        )

    def first_copies(j, half, d):
        if d == 2:
            return [
                ring_copy(j, half, 2, low, hop.at[j, half, 0], s1_send, h_recv, after),
                ring_copy(j, half, 2, high, hop.at[j, half, 1], s1_send, h_recv, before),
            ]
        if d == after:
            return [ring_copy(j, half, d, high, got1.at[j, half, 0, high], s1_send, s1_recv, d)]
        if d == before:
            return [ring_copy(j, half, d, low, got1.at[j, half, 1, low], s1_send, s1_recv, d)]
        return []

    def hop_wait(j):
        wait(hop.at[j], h_recv.at[j])

    def stage_hop(j):
        hop_wait(j)
        for half in range(2):
            for n, d, part_of in ((0, after, low), (1, before, high)):
                lead = lead_of(half, d)
                total = dense[j, half, lead, part_of].astype(F32) + hop[j, half, n].astype(F32)
                dense[j, half, lead, part_of] = total.astype(BF16)
                ring_copy(j, half, d, part_of, got1.at[j, half, n, part_of], b_send, s1_recv, d).start()

    def second_copies(j, half, d):
        o = lax.rem(place[1 - half] + d, 4)
        return [
            remote(
                part.at[j, half, o, h], got2.at[j, half, d, core],
                s2_send.at[j], s2_recv.at[j], (r, whom[1 - half](o, h)),
            )
            for h in (core, 1 - core)[0 if d else 1:]
        ]

    def t_wait(j):
        wait(terms[j].at[pl.ds(0, NONE)], t_recv.at[j])

    def first_wait(j):
        wait(got1.at[j], s1_recv.at[j])

    def second_wait(j):
        wait(got2.at[j], s2_recv.at[j])

    def stage0(j):
        t_wait(j)
        for d in (2, 1, 3, 0):
            for half in range(2):
                sum_terms(j, half, lax.rem(place[half] + d, 4))
                for copy in first_copies(j, half, d):
                    copy.start()

    def stage1(j):
        t_drain(j)
        first_wait(j)
        for half in range(2):
            for d in (2, 1, 3, 0):
                o = lax.rem(place[1 - half] + d, 4)
                total = dense[j, half, place[half], o].astype(F32)
                for e in range(2):
                    total += got1[j, half, e, o].astype(F32)
                part[j, half, o] = total.astype(BF16)
                for copy in second_copies(j, half, d):
                    copy.start()
            pltpu.make_async_copy(
                part.at[j, half, place[1 - half], core], got2.at[j, half, 0, core], s2_recv.at[j]
            ).start()

    def second_drain(j):
        wait(terms[j].at[pl.ds(0, 7)], s2_send.at[j])

    def stage2(j):
        wait(got1.at[j], s1_send.at[j])
        wait(hop.at[j], b_send.at[j])
        if j:
            second_drain(j - 1)
        second_wait(j)
        for half in range(2):
            total = got2[j, half, 0].astype(F32)
            for d in (1, 2, 3):
                total += got2[j, half, d].astype(F32)
            total = total.astype(BF16)
            for h in range(2):
                diag[0, pl.ds(h * HF + j * CR, CR), columns[half]] = total[h]

    for j in range(CH + 3):
        if j < CH:
            stage0(j)
        if j == X_AT:
            x_start()
        if 1 <= j <= CH:
            stage_hop(j - 1)
        if 2 <= j <= CH + 1:
            stage1(j - 2)
        if j >= 3:
            stage2(j - 3)

    def x_wait():
        wait(cross, x_recv)

    x_wait()
    second_drain(CH - 1)
    wait(cross.at[pl.ds(0, 3)], x_send.at[1])

    @pl.when(owner)
    def _():
        wait(cross.at[pl.ds(0, 3)], x_send.at[0])

    @pl.when(r == back)
    def _():
        wait(x_relay, xr_send)


def store(cross, diag, cross_out, diag_out, sem):
    copies = [pltpu.make_async_copy(cross.at[b], cross_out.at[b], sem.at[b]) for b in range(NB)]
    copies.append(pltpu.make_async_copy(diag, diag_out, sem.at[NB]))
    for copy in copies:
        copy.start()
    for copy in copies:
        copy.wait()


def per_device(stiffness, coupling, slave_diag, slave_masters):
    any_space = pl.BlockSpec(memory_space=pl.ANY)
    vmem = pl.BlockSpec(memory_space=pltpu.VMEM)
    dma = pltpu.SemaphoreType.DMA
    flops = 2 * NB * (2 * NS * NS * FW + 3 * FW * FW * NS) // 4
    cross, diag = pl.pallas_call(
        kernel,
        out_shape=(pltpu.VMEM((NB, QF, FW), BF16), pltpu.VMEM((1, QF, FW), BF16)),
        in_specs=[any_space] * 4,
        out_specs=(vmem, vmem),
        scratch_shapes=[
            pltpu.VMEM((2, NS, NS), BF16),
            pltpu.VMEM((2, 2 * FW, NS), BF16),
            pltpu.VMEM((NB, QN, 2, FW), BF16),
            pltpu.VMEM((NB, QN), F32),
            pltpu.VMEM((2, NB), jnp.int32),
            pltpu.VMEM((NB, 2 * FW, QN), BF16),
            pltpu.VMEM((2 * FW, QN), BF16),
            pltpu.VMEM((QF, FW), BF16),
            pltpu.VMEM((2, FW, NS), BF16),
            pltpu.VMEM((2, 3, FW, FW), BF16),
            pltpu.VMEM((CH, 2, 4, 4, 2, CR, HC), BF16),
            pltpu.VMEM((CH, 2, 2, 2, 2, CR, HC), BF16),
            pltpu.VMEM((CH, 2, 2, 4, 2, CR, HC), BF16),
            pltpu.VMEM((CH, 2, 4, 2, CR, HC), BF16),
            pltpu.VMEM((CH, 2, 4, 2, CR, HC), BF16),
            pltpu.VMEM((2, 8, 128), jnp.int32),
            pltpu.VMEM((2, 2, 8, 128), jnp.int32),
            pltpu.SMEM((2, 2, 8, 128), jnp.int32),
            dma((2,)), dma((2,)), dma((NB,)), dma((2,)), dma((2, 2)), dma, dma((2,)),
            dma((2, CH)), dma((CH,)), dma((2,)), dma, dma, dma,
            dma((CH,)), dma((CH,)), dma((CH,)), dma((CH,)), dma((CH,)), dma((CH,)), dma((2,)), dma, dma,
            dma((2,)), pltpu.SemaphoreType.REGULAR((2,)),
            *[pltpu.VMEM((NONE + 1, CR, FW), BF16)] * CH,
        ],
        compiler_params=pltpu.CompilerParams(
            collective_id=0, has_side_effects=True, vmem_limit_bytes=58 * 2**20
        ),
        cost_estimate=pl.CostEstimate(flops=flops, bytes_accessed=9 * 2**20, transcendentals=0),
        name="condense",
    )(stiffness, coupling, slave_diag, slave_masters.T)
    cross = pltpu.with_memory_space_constraint(cross, pltpu.VMEM)
    diag = pltpu.with_memory_space_constraint(diag, pltpu.VMEM)
    return pl.pallas_call(
        store,
        out_shape=(
            jax.ShapeDtypeStruct((NB, QF, FW), BF16),
            jax.ShapeDtypeStruct((1, QF, FW), BF16),
        ),
        in_specs=[vmem, vmem],
        out_specs=(any_space, any_space),
        scratch_shapes=[dma((NB + 1,))],
        cost_estimate=pl.CostEstimate(flops=0, bytes_accessed=4 * 2**20, transcendentals=0),
        name="store",
    )(cross, diag)


def solution(mesh):
    return jax.shard_map(
        per_device,
        mesh=mesh,
        in_specs=(
            P("col", "row", None),
            P("col", "row", None, None),
            P("col", "row"),
            P("col", None),
        ),
        out_specs=(P("col", "row", None), P("col", "row", None)),
        check_vma=False,
    )
```

```python
import functools

import jax
import jax.numpy as jnp
from jax import lax
from jax.experimental import pallas as pl
from jax.experimental.pallas import tpu as pltpu
from jax.sharding import PartitionSpec as P

MESH = pl.DeviceIdType.MESH
F32 = jnp.float32
BF16 = jnp.bfloat16
ROWS = 4
NB = 5
QN = 256
NS = 1024
FW = 768
QF = FW // ROWS
HF = QF // 2
HC = FW // 2
NONE = 4 * NB
CH = 6
CR = HF // CH
X_AT = 4


def kernel(
    stiff, coup, scale_in, masters_in,
    cross, diag,
    kbuf, pbuf, cin, scale, masters, ploc, relay, x_relay, left, fills, dense, hop, got1, part, got2,
    own_table, idx_v, idx_s,
    k_send, k_recv, c_sem, p_send, p_recv, r_send, r_recv, t_send, t_recv, x_send, x_recv, xr_send, xr_recv,
    s1_send, s1_recv, s2_send, s2_recv, h_recv, b_send, i_sem, i_send, i_recv, small, ready, *terms,
):
    r = lax.axis_index("row")
    c = lax.axis_index("col")
    core = lax.rem(c, 2)
    y = lax.rem(c // 2, 4)
    z = c // 8
    other = c + 1 - 2 * core
    target = 2 * core
    through = target + 1
    far = lax.rem(target + 2, ROWS)
    back = lax.rem(target + 3, ROWS)

    def at_y(v, h=core):
        return z * 8 + v * 2 + h

    def at_z(v, h=core):
        return v * 8 + y * 2 + h

    def wait(ref, sem):
        pltpu.make_async_copy(ref, ref, sem).wait()

    def remote(src, dst, send, recv, device):
        return pltpu.make_async_remote_copy(
            src_ref=src, dst_ref=dst, send_sem=send, recv_sem=recv, device_id=device, device_id_type=MESH
        )

    barrier = pltpu.get_barrier_semaphore()
    partners = [(r, other)]
    for d in (1, 2, 3):
        row = lax.rem(r + d, ROWS)
        partners += [(row, c), (row, other)]
        for h in (core, 1 - core):
            partners += [(r, at_y(lax.rem(y + d, 4), h)), (r, at_z(lax.rem(z + d, 4), h))]
    for device in partners:
        pl.semaphore_signal(barrier, inc=1, device_id=device, device_id_type=MESH)
    order = [4] + [lax.rem(r + d, ROWS) for d in (1, 2, 3, 0)]
    loads = [pltpu.make_async_copy(coup.at[b], cin.at[b], c_sem.at[i]) for i, b in enumerate(order)]
    for load in loads:
        load.start()
    small_loads = [
        pltpu.make_async_copy(scale_in, scale, small.at[0]), pltpu.make_async_copy(masters_in, masters, small.at[1])
    ]
    for load in small_loads:
        load.start()

    for load in small_loads:
        load.wait()
    lane = lax.broadcasted_iota(jnp.int32, (8, 128), 1)
    least, most = jnp.full((8, 128), NONE, jnp.int32), jnp.full((8, 128), -1, jnp.int32)
    for e in range(2 * NB):
        hit = lane == jnp.broadcast_to(masters[pl.ds(e % 2, 1), pl.ds(e // 2, 1)], (8, 128))
        least = jnp.minimum(least, jnp.where(hit, core * 2 * NB + e, NONE))
        most = jnp.maximum(most, jnp.where(hit, core * 2 * NB + e, -1))
    own_table[0] = least
    own_table[1] = jnp.where(most > least, most, NONE)

    mine = pl.ds(pl.multiple_of(r * QN, QN), QN)

    def k_copy(b, slot, row):
        return remote(stiff.at[b], kbuf.at[slot, mine], k_send.at[slot], k_recv.at[slot], (row, c))

    def k_local(b, slot):
        return pltpu.make_async_copy(stiff.at[b], kbuf.at[slot, mine], k_recv.at[slot])

    def p_copy(b, slot, row, k):
        return remote(
            ploc.at[b, pl.ds(k * FW, FW)], pbuf.at[slot, pl.ds(k * FW, FW), mine],
            p_send.at[slot], p_recv.at[slot, k], (row, c),
        )

    def p_aside(k):
        return remote(
            ploc.at[4, pl.ds(k * FW, FW)], relay.at[pl.ds(k * FW, FW)],
            p_send.at[0], r_recv.at[k], (through, c),
        )

    def p_forward(k):
        return remote(
            relay.at[pl.ds(k * FW, FW)],
            pbuf.at[0, pl.ds(k * FW, FW), pl.ds(pl.multiple_of(far * QN, QN), QN)],
            r_send, p_recv.at[0, k], (target, c),
        )

    def p_local(b, slot, k):
        return pltpu.make_async_copy(
            ploc.at[b, pl.ds(k * FW, FW)], pbuf.at[slot, pl.ds(k * FW, FW), mine], p_recv.at[slot, k]
        )

    def send_block(i, remote_copy, local_copy, aside=None):
        if i == 0:
            @pl.when(r == target)
            def _():
                local_copy(4, 0).start()

            @pl.when((r != target) & (r != far if aside else True))
            def _():
                remote_copy(4, 0, target).start()

            if aside:
                @pl.when(r == far)
                def _():
                    aside().start()
        elif i == 3:
            @pl.when(r != through)
            def _():
                remote_copy(order[i], 1, order[i]).start()
        elif i < 4:
            remote_copy(order[i], 1, order[i]).start()
        else:
            local_copy(order[i], 1).start()

    def project(i, k):
        b = order[i]
        if k == 0:
            loads[i].wait()
        raw = cin[b, :, k, :].astype(F32).T
        ploc[b, pl.ds(k * FW, FW), :] = (raw / scale[pl.ds(b, 1), :]).astype(BF16)

    def p_start(i, k):
        send_block(
            i, functools.partial(p_copy, k=k), functools.partial(p_local, k=k), functools.partial(p_aside, k)
        )

    project(0, 0)
    project(0, 1)
    pl.semaphore_wait(barrier, len(partners))
    send_block(0, k_copy, k_local)
    p_start(0, 0)
    p_start(0, 1)
    for i in range(1, NB):
        send_block(i, k_copy, k_local)
    for k in range(2):
        for i in range(1, NB):
            project(i, k)
            p_start(i, k)

    own_idx = pltpu.make_async_copy(own_table, idx_v.at[core], i_sem.at[0])
    own_idx.start()
    idx_copy = remote(own_table, idx_v.at[core], i_send, i_recv, (r, other))
    idx_copy.start()

    for chunk in terms:
        chunk[NONE] = jnp.zeros((CR, FW), BF16)
    own_idx.wait()
    idx_copy.wait()
    to_smem = pltpu.make_async_copy(idx_v, idx_s, i_sem.at[1])
    to_smem.start()
    to_smem.wait()

    @pl.when(r == through)
    def _():
        for k in range(2):
            wait(relay.at[pl.ds(k * FW, FW)], r_recv.at[k])
            p_forward(k).start()
        k_copy(order[3], 1, order[3]).start()
        for k in range(2):
            p_copy(order[3], 1, order[3], k).start()

    def t_copies(slot, b, f, j):
        at = core * 2 * NB + b * 2 + f
        copies = []
        for dq in range(ROWS):
            for dh in range(2):
                q, h = lax.rem(r + dq, ROWS), lax.rem(core + dh, 2)
                src = fills.at[slot, f, pl.ds(pl.multiple_of(q * QF + h * HF + j * CR, CR), CR)]
                dst = terms[j].at[at]
                if dq or dh:
                    copies.append(remote(
                        src, dst, t_send.at[slot, j], t_recv.at[j], (q, c - core + h)
                    ))
                else:
                    copies.append(pltpu.make_async_copy(src, dst, t_recv.at[j]))
        return copies

    def x_aside():
        src = fills.at[0, 2, pl.ds(pl.multiple_of(far * QF, QF), QF)]
        return remote(src, x_relay, x_send.at[0], xr_recv, (back, c))

    def x_forward():
        return remote(x_relay, cross.at[4], xr_send, x_recv, (far, c))

    def x_copies(slot, b):
        copies = []
        for dq in range(ROWS):
            if slot == 0 and dq == 2:
                continue
            q = lax.rem(r + dq, ROWS)
            src = fills.at[slot, 2, pl.ds(pl.multiple_of(q * QF, QF), QF)]
            if dq:
                copies.append(remote(src, cross.at[b], x_send.at[slot], x_recv, (q, c)))
            else:
                copies.append(pltpu.make_async_copy(src, cross.at[b], x_recv))
        return copies

    def fill(slot, f, a, b, skip=False):
        for n in range(3):
            out = lax.dot_general(
                left[a], pbuf[slot, pl.ds(b * FW + n * 256, 256), :],
                (((1,), (1,)), ((), ())), preferred_element_type=F32,
            ).astype(BF16)
            if skip:
                for q in range(2 * ROWS):
                    fills[slot, f, pl.ds(q * HF + CR, HF - CR), pl.ds(n * 256, 256)] = out[q * HF + CR:(q + 1) * HF]
            else:
                fills[slot, f, :, pl.ds(n * 256, 256)] = out

    def fill_head(f):
        rows = [pbuf[1, pl.ds(f * FW + q * HF, CR), :] for q in range(2 * ROWS)]
        head = jnp.dot(jnp.concatenate(rows), kbuf[1], preferred_element_type=F32).astype(BF16)
        out = lax.dot_general(
            head, pbuf[1, pl.ds(f * FW, FW), :], (((1,), (1,)), ((), ())), preferred_element_type=F32
        ).astype(BF16)
        for q in range(2 * ROWS):
            fills[1, f, pl.ds(q * HF, CR), :] = out[q * CR:(q + 1) * CR]

    def multiply(slot, k):
        for n in range(4):
            out = jnp.dot(
                pbuf[slot, pl.ds(k * FW, FW), :], kbuf[slot, :, pl.ds(n * 256, 256)],
                preferred_element_type=F32,
            )
            left[k, :, pl.ds(n * 256, 256)] = out.astype(BF16)

    def block(slot, unused):
        b = jnp.where(slot == 0, 4, r)

        def p_wait(k):
            wait(pbuf.at[slot, pl.ds(k * FW, FW)], p_recv.at[slot, k])

        def t_start(f, j):
            for copy in t_copies(slot, b, f, j):
                copy.start()

        def k_wait():
            wait(kbuf.at[slot], k_recv.at[slot])

        def tell(stage):
            for device in ring:
                pl.semaphore_signal(ready.at[stage], inc=1, device_id=device, device_id_type=MESH)

        k_wait()
        p_wait(0)
        multiply(slot, 0)
        fill(slot, 0, 0, 0)

        @pl.when(owner & (slot == 1))
        def _():
            tell(0)
            t_start(0, 0)
            p_wait(1)
            tell(1)
            fill_head(1)
            t_start(1, 0)
            multiply(slot, 1)
            fill(slot, 1, 1, 1, skip=True)

        @pl.when(jnp.logical_not(owner & (slot == 1)))
        def _():
            p_wait(1)
            multiply(slot, 1)
            fill(slot, 1, 1, 1)

            @pl.when(jnp.logical_not(owner))
            def _():
                fill(slot, 2, 0, 1)
                pl.semaphore_wait(ready.at[0], 2)

            t_start(0, 0)
            t_start(1, 0)

            @pl.when(jnp.logical_not(owner))
            def _():
                pl.semaphore_wait(ready.at[1], 2)

        for j in range(1, CH):
            for f in range(2):
                t_start(f, j)

        @pl.when(owner)
        def _():
            fill(slot, 2, 0, 1)

        @pl.when(slot == 0)
        def _():
            x_aside().start()

        return unused

    owner = r == target
    def k_drain():
        wait(kbuf.at[1, pl.ds(0, 3 * QN)], k_send.at[1])
        wait(pbuf.at[1, pl.ds(0, 3 * FW // 2)], p_send.at[1])

        @pl.when(r != target)
        def _():
            wait(kbuf.at[1, pl.ds(0, QN)], k_send.at[0])
            wait(ploc.at[4], p_send.at[0])

        @pl.when(r == through)
        def _():
            wait(relay, r_send)

    def t_drain(j):
        def one(slot, unused):
            wait(terms[j].at[pl.ds(0, 14)], t_send.at[slot, j])
            return unused

        lax.fori_loop(first_slot, 2, one, 0)

    first_slot = jnp.where(owner, 0, 1)
    ring = [(r, other)] + [(lax.rem(r + d, ROWS), col) for d in (1, 2, 3) for col in (c, other)]
    lax.fori_loop(first_slot, 2, block, 0)

    @pl.when(owner)
    def _():
        for stage in range(2):
            pl.semaphore_wait(ready.at[stage], 1)

    def x_start():
        for copy in x_copies(1, r):
            copy.start()

        @pl.when(owner)
        def _():
            for copy in x_copies(0, 4):
                copy.start()

        @pl.when(r == back)
        def _():
            wait(x_relay, xr_recv)
            x_forward().start()

    k_drain()


    place = (y, z)
    whom = (at_y, at_z)
    columns = (pl.ds(0, HC), pl.ds(HC, HC))

    def sum_terms(j, half, lead):
        chunk, cols = terms[j], columns[half]

        def one(n, unused):
            o, h = n // 2, lax.rem(n, 2)
            zz, yy = (o, lead) if half == 0 else (lead, o)
            m = zz * 8 + yy * 2 + h
            total = chunk[idx_s[0, 0, 0, m], :, cols].astype(F32) + chunk[idx_s[0, 1, 0, m], :, cols].astype(F32)
            total += chunk[idx_s[1, 0, 0, m], :, cols].astype(F32) + chunk[idx_s[1, 1, 0, m], :, cols].astype(F32)
            dense[j, half, lead, o, h] = total.astype(BF16)
            return unused

        lax.fori_loop(0, 8, one, 0)

    after, before, low, high = 1, 3, pl.ds(0, 2), pl.ds(2, 2)

    def lead_of(half, d):
        return lax.rem(place[half] + d, 4)

    def ring_copy(j, half, lead, part_of, dst, send, recv, d):
        return remote(
            dense.at[j, half, lead_of(half, lead), part_of], dst, send.at[j], recv.at[j],
            (r, whom[half](lead_of(half, d))),
        )

    def first_copies(j, half, d):
        if d == 2:
            return [
                ring_copy(j, half, 2, low, hop.at[j, half, 0], s1_send, h_recv, after),
                ring_copy(j, half, 2, high, hop.at[j, half, 1], s1_send, h_recv, before),
            ]
        if d == after:
            return [ring_copy(j, half, d, high, got1.at[j, half, 0, high], s1_send, s1_recv, d)]
        if d == before:
            return [ring_copy(j, half, d, low, got1.at[j, half, 1, low], s1_send, s1_recv, d)]
        return []

    def hop_wait(j):
        wait(hop.at[j], h_recv.at[j])

    def stage_hop(j):
        hop_wait(j)
        for half in range(2):
            for n, d, part_of in ((0, after, low), (1, before, high)):
                lead = lead_of(half, d)
                total = dense[j, half, lead, part_of].astype(F32) + hop[j, half, n].astype(F32)
                dense[j, half, lead, part_of] = total.astype(BF16)
                ring_copy(j, half, d, part_of, got1.at[j, half, n, part_of], b_send, s1_recv, d).start()

    def second_copies(j, half, d):
        o = lax.rem(place[1 - half] + d, 4)
        return [
            remote(
                part.at[j, half, o, h], got2.at[j, half, d, core],
                s2_send.at[j], s2_recv.at[j], (r, whom[1 - half](o, h)),
            )
            for h in (core, 1 - core)[0 if d else 1:]
        ]

    def t_wait(j):
        wait(terms[j].at[pl.ds(0, NONE)], t_recv.at[j])

    def first_wait(j):
        wait(got1.at[j], s1_recv.at[j])

    def second_wait(j):
        wait(got2.at[j], s2_recv.at[j])

    def stage0(j):
        t_wait(j)
        for d in (2, 1, 3, 0):
            for half in range(2):
                sum_terms(j, half, lax.rem(place[half] + d, 4))
                for copy in first_copies(j, half, d):
                    copy.start()

    def stage1(j):
        t_drain(j)
        first_wait(j)
        for half in range(2):
            for d in (2, 1, 3, 0):
                o = lax.rem(place[1 - half] + d, 4)
                total = dense[j, half, place[half], o].astype(F32)
                for e in range(2):
                    total += got1[j, half, e, o].astype(F32)
                part[j, half, o] = total.astype(BF16)
                for copy in second_copies(j, half, d):
                    copy.start()
            pltpu.make_async_copy(
                part.at[j, half, place[1 - half], core], got2.at[j, half, 0, core], s2_recv.at[j]
            ).start()

    def second_drain(j):
        wait(terms[j].at[pl.ds(0, 7)], s2_send.at[j])

    def stage2(j):
        wait(got1.at[j], s1_send.at[j])
        wait(hop.at[j], b_send.at[j])
        if j:
            second_drain(j - 1)
        second_wait(j)
        for half in range(2):
            total = got2[j, half, 0].astype(F32)
            for d in (1, 2, 3):
                total += got2[j, half, d].astype(F32)
            total = total.astype(BF16)
            for h in range(2):
                diag[0, pl.ds(h * HF + j * CR, CR), columns[half]] = total[h]

    for j in range(CH + 3):
        if j < CH:
            stage0(j)
        if j == X_AT:
            x_start()
        if 1 <= j <= CH:
            stage_hop(j - 1)
        if 2 <= j <= CH + 1:
            stage1(j - 2)
        if j >= 3:
            stage2(j - 3)

    def x_wait():
        wait(cross, x_recv)

    x_wait()
    second_drain(CH - 1)
    wait(cross.at[pl.ds(0, 3)], x_send.at[1])

    @pl.when(owner)
    def _():
        wait(cross.at[pl.ds(0, 3)], x_send.at[0])

    @pl.when(r == back)
    def _():
        wait(x_relay, xr_send)


def store(cross, diag, cross_out, diag_out, sem):
    copies = []
    for h in range(2):
        rows = pl.ds(h * HF, HF)
        for b in range(NB):
            copies.append(pltpu.make_async_copy(cross.at[b, rows], cross_out.at[b, rows], sem.at[h, b]))
        copies.append(pltpu.make_async_copy(diag.at[0, rows], diag_out.at[0, rows], sem.at[h, NB]))
    for copy in copies:
        copy.start()
    for copy in copies:
        copy.wait()


def per_device(stiffness, coupling, slave_diag, slave_masters):
    any_space = pl.BlockSpec(memory_space=pl.ANY)
    vmem = pl.BlockSpec(memory_space=pltpu.VMEM)
    dma = pltpu.SemaphoreType.DMA
    flops = 2 * NB * (2 * NS * NS * FW + 3 * FW * FW * NS) // 4
    cross, diag = pl.pallas_call(
        kernel,
        out_shape=(pltpu.VMEM((NB, QF, FW), BF16), pltpu.VMEM((1, QF, FW), BF16)),
        in_specs=[any_space] * 4,
        out_specs=(vmem, vmem),
        scratch_shapes=[
            pltpu.VMEM((2, NS, NS), BF16),
            pltpu.VMEM((2, 2 * FW, NS), BF16),
            pltpu.VMEM((NB, QN, 2, FW), BF16),
            pltpu.VMEM((NB, QN), F32),
            pltpu.VMEM((2, NB), jnp.int32),
            pltpu.VMEM((NB, 2 * FW, QN), BF16),
            pltpu.VMEM((2 * FW, QN), BF16),
            pltpu.VMEM((QF, FW), BF16),
            pltpu.VMEM((2, FW, NS), BF16),
            pltpu.VMEM((2, 3, FW, FW), BF16),
            pltpu.VMEM((CH, 2, 4, 4, 2, CR, HC), BF16),
            pltpu.VMEM((CH, 2, 2, 2, 2, CR, HC), BF16),
            pltpu.VMEM((CH, 2, 2, 4, 2, CR, HC), BF16),
            pltpu.VMEM((CH, 2, 4, 2, CR, HC), BF16),
            pltpu.VMEM((CH, 2, 4, 2, CR, HC), BF16),
            pltpu.VMEM((2, 8, 128), jnp.int32),
            pltpu.VMEM((2, 2, 8, 128), jnp.int32),
            pltpu.SMEM((2, 2, 8, 128), jnp.int32),
            dma((2,)), dma((2,)), dma((NB,)), dma((2,)), dma((2, 2)), dma, dma((2,)),
            dma((2, CH)), dma((CH,)), dma((2,)), dma, dma, dma,
            dma((CH,)), dma((CH,)), dma((CH,)), dma((CH,)), dma((CH,)), dma((CH,)), dma((2,)), dma, dma,
            dma((2,)), pltpu.SemaphoreType.REGULAR((2,)),
            *[pltpu.VMEM((NONE + 1, CR, FW), BF16)] * CH,
        ],
        compiler_params=pltpu.CompilerParams(
            collective_id=0, has_side_effects=True, vmem_limit_bytes=58 * 2**20
        ),
        cost_estimate=pl.CostEstimate(flops=flops, bytes_accessed=9 * 2**20, transcendentals=0),
        name="condense",
    )(stiffness, coupling, slave_diag, slave_masters.T)
    cross = pltpu.with_memory_space_constraint(cross, pltpu.VMEM)
    diag = pltpu.with_memory_space_constraint(diag, pltpu.VMEM)
    return pl.pallas_call(
        store,
        out_shape=(
            jax.ShapeDtypeStruct((NB, QF, FW), BF16),
            jax.ShapeDtypeStruct((1, QF, FW), BF16),
        ),
        in_specs=[vmem, vmem],
        out_specs=(any_space, any_space),
        scratch_shapes=[dma((2, NB + 1))],
        cost_estimate=pl.CostEstimate(flops=0, bytes_accessed=4 * 2**20, transcendentals=0),
        name="store",
    )(cross, diag)


def solution(mesh):
    return jax.shard_map(
        per_device,
        mesh=mesh,
        in_specs=(
            P("col", "row", None),
            P("col", "row", None, None),
            P("col", "row"),
            P("col", None),
        ),
        out_specs=(P("col", "row", None), P("col", "row", None)),
        check_vma=False,
    )
```
